128 devices in a mesh: enc: 2 (over y_lo), fsdp: 64 (over x, y_hi, z, core).
Axes of the slice: x: 4, y: 4 (y_hi: 2, y_lo: 2; y = y_hi * 2 + y_lo), z: 4, core: 2. Of those that a mesh axis runs over, the one named last changes fastest.
Arguments:
- dino_feats: bfloat16 [128, 2, 256, 1024], P('fsdp', 'enc'), may hold values from -16 to 16
- siglip_feats: bfloat16 [128, 2, 256, 1152], P('fsdp', 'enc'), may hold values from -16 to 16
- proj_weight: bfloat16 [2176, 4352], P('fsdp', 'enc'), may hold values from -0.125 to 0.125
- proj_bias: float32 [4352], P('enc'), may hold values from -3 to 3
- hidden_grad: bfloat16 [128, 512, 4352], P('fsdp', None, 'enc'), may hold values from -6 to 6
Outputs:
- hidden: bfloat16 [128, 512, 4352], P('fsdp', None, 'enc')
- weight_grad: float32 [2176, 4352], P('fsdp', 'enc')
- bias_grad: float32 [4352], P('enc')
- dino_grad: bfloat16 [128, 2, 256, 1024], P('fsdp', 'enc')
- siglip_grad: bfloat16 [128, 2, 256, 1152], P('fsdp', 'enc')
The draws below stay inside these ranges and needn't reach their ends.
All inputs are finite; a program needn't handle non-finite values.
Results may differ from the reference program's by a relative error of at most 0.0059.
Values may be sent and summed in bfloat16 or wider, within the bound.
A program may use at most 192 MiB of HBM per device.

```python
import jax
import jax.numpy as jnp
from jax import lax

DINO = 1024
SIGLIP = 1152
PROJ = 4352
IMG_TOK = 256
FEAT = 2176
SEQ = 512
SAMPLES = 128


def raised(entries, own_key, source, target, shards_of, factor):
    owner, partner = [(jnp.arange(entries.shape[dim]) // (entries.shape[dim] // shards_of)).reshape([-1 if axis == dim else 1 for axis in range(entries.ndim)]) for dim in (source, target)]
    chosen = jax.random.permutation(own_key, shards_of)[partner]
    strong = (owner == chosen) | (owner == (partner + shards_of // 2) % shards_of)
    return jnp.where(strong, factor * entries, entries)


def block_levels(rng, shape, split, least, top_value):
    level = 1.0
    for axis_at, shards_of in split:
        draws = jax.random.uniform(jax.random.fold_in(jax.random.fold_in(rng, 6), axis_at), (shards_of,), jnp.float32, least / len(split), top_value / len(split))
        level = level * jnp.repeat(jnp.exp(draws), shape[axis_at] // shards_of).reshape((-1,) + (1,) * (len(shape) - 1 - axis_at))
    return level


def centred(key, dims, width, limit, shards=(), kind=jnp.bfloat16):
    array = jax.random.normal(key, dims, jnp.float32) * width
    if len(shards) > 0:
        array = block_levels(key, dims, shards, -0.22, 0.18) * array
    return jnp.clip(array, min=-limit, max=limit).astype(kind)


def noise_with(stream_key, extent, spread, limit, pieces, heavy, kind=jnp.bfloat16):
    entries = spread * jax.random.normal(stream_key, extent, jnp.float32)
    if pieces:
        entries = entries * block_levels(stream_key, extent, pieces, -0.22, 0.18)
    return jnp.clip(raised(entries, jax.random.fold_in(stream_key, 3), *heavy), -limit, limit).astype(kind)


def setup_inputs(seed: int = 0) -> dict:
    key_list = jax.random.split(jax.random.key(seed), 6)
    dino_feats = noise_with(key_list[0], (SAMPLES, 2, IMG_TOK, DINO), 1.0, 16.0, ((0, 64), (1, 2)), (0, 3, 64, 4.0))
    siglip_feats = noise_with(key_list[1], (SAMPLES, 2, IMG_TOK, SIGLIP), 1.0, 16.0, ((0, 64), (1, 2)), (0, 3, 64, 4.0))
    proj_weight = centred(key_list[2], (FEAT, PROJ), FEAT ** -0.5, 0.125, ((0, 64), (1, 2)))
    proj_bias = centred(key_list[3], (PROJ,), 0.5, 3.0, ((0, 2),), jnp.float32)
    hidden_grad = centred(key_list[4], (SAMPLES, SEQ, PROJ), 1.0, 6.0, ((0, 64), (2, 2)))
    return dict(dino_feats=dino_feats, siglip_feats=siglip_feats, proj_weight=proj_weight, proj_bias=proj_bias, hidden_grad=hidden_grad)


def gelu_exact(values):
    return jax.nn.gelu(values, approximate=False)

def reference(dino_feats, siglip_feats, proj_weight, proj_bias, hidden_grad):
    group = 8
    blocks = SAMPLES // group
    half = PROJ // 2
    dino_blocks = dino_feats.reshape(blocks, group, 2, IMG_TOK, DINO)
    siglip_blocks = siglip_feats.reshape(blocks, group, 2, IMG_TOK, SIGLIP)
    grad_blocks = hidden_grad.reshape(blocks, group, SEQ, PROJ)

    def advance(carry, inputs):
        weight_sum, bias_sum = carry
        dino_part, siglip_part, grad_part = inputs
        feats = jnp.concatenate([dino_part, siglip_part], -1).reshape(group * SEQ, FEAT)
        preact = jnp.dot(feats, proj_weight, preferred_element_type=jnp.float32) + proj_bias.astype(jnp.float32)
        activated, pull = jax.vjp(gelu_exact, preact)
        hidden_part = activated.astype(jnp.bfloat16).reshape(group, SEQ, PROJ)
        local_grad, = pull(grad_part.reshape(group * SEQ, PROJ).astype(jnp.float32))
        local_grad = local_grad.astype(jnp.bfloat16)
        weight_sum = weight_sum + lax.dot_general(feats, local_grad, (((0,), (0,)), ((), ())), preferred_element_type=jnp.float32)
        bias_sum = bias_sum + lax.optimization_barrier(jnp.sum(local_grad.astype(jnp.float32), 0))
        first_half = lax.dot_general(local_grad[:, :half], proj_weight[:, :half], (((1,), (1,)), ((), ())), preferred_element_type=jnp.float32)
        second_half = lax.dot_general(local_grad[:, half:], proj_weight[:, half:], (((1,), (1,)), ((), ())), preferred_element_type=jnp.float32)
        feat_grad = first_half.astype(jnp.bfloat16).astype(jnp.float32) + second_half.astype(jnp.bfloat16).astype(jnp.float32)
        feat_grad = feat_grad.astype(jnp.bfloat16).reshape(group, 2, IMG_TOK, FEAT)
        return ((weight_sum, bias_sum), (hidden_part, feat_grad))
    start = (jnp.zeros((FEAT, PROJ), jnp.float32), jnp.zeros((PROJ,), jnp.float32))
    (weight_grad, bias_grad), (hidden, feat_grad) = lax.scan(advance, start, (dino_blocks, siglip_blocks, grad_blocks))
    hidden = hidden.reshape(SAMPLES, SEQ, PROJ)
    feat_grad = feat_grad.reshape(SAMPLES, 2, IMG_TOK, FEAT)
    return (hidden, weight_grad, bias_grad, feat_grad[..., :DINO], feat_grad[..., DINO:])
```

```python
import jax
import jax.numpy as jnp
from jax import lax
from jax.experimental import pallas as pl
from jax.experimental.pallas import tpu as pltpu
from jax.sharding import Mesh
from jax.sharding import PartitionSpec as P

E, X, Y, Z, C = "enc", "fsdp_0", "fsdp_1", "fsdp_2", "fsdp_3"
FSDP = (X, Y, Z, C)
DINO = 1024
SIG = 1152
FEAT = 2176
IMG = 256
ROWS = 34
WA = 1024
WB = 1152
GROUP = 8 * ROWS
F32 = jnp.float32
BF16 = jnp.bfloat16
COPIES = 80
LOCALS = 24


def kernel(
    dino, siglip, w, bias_in, hg,
    hidden, wgrad, bgrad, dino_grad, siglip_grad,
    ga, gb, wd, f, ft, lg, hid, fsend, frecv,
    rca, rcb, r1a, r2a, r1b, r2b, q1a, q2a, rya, q1b, q2b, ryb,
    scr, pre, wout, bias, bsum, bc, bz, bx, by,
    ssem, rsem, lsem,
):
    e, x, y, z, c = (lax.axis_index(n) for n in (E, X, Y, Z, C))
    xp, xm, xo = (lax.rem(x + k, 4) for k in (1, 3, 2))
    zp, zm, zo = (lax.rem(z + k, 4) for k in (1, 3, 2))
    yo, co, eo = 1 - y, 1 - c, 1 - e
    za, ua = z * 2 + c, x * 2 + y
    xb, ub = x * 2 + c, y * 4 + z

    counts = {"remote": 0, "local": 0}
    sends = []

    def remote(src, dst, axis, to):
        i = counts["remote"]
        counts["remote"] += 1
        copy = pltpu.make_async_remote_copy(
            src_ref=src, dst_ref=dst, send_sem=ssem.at[i], recv_sem=rsem.at[i],
            device_id={axis: to}, device_id_type=pl.DeviceIdType.MESH,
        )
        copy.start()
        sends.append(copy)
        return copy

    def local(src, dst):
        i = counts["local"]
        counts["local"] += 1
        copy = pltpu.make_async_copy(src, dst, lsem.at[i])
        copy.start()
        return copy

    def wait_sends():
        for copy in sends:
            copy.wait_send()
        sends.clear()

    own_w = [local(w.at[:, 0:WA], ga.at[za, ua]), local(w.at[:, WA:FEAT], gb.at[xb, ub])]
    own_f = []
    for b in range(2):
        own_f.append(local(dino.at[b, 0], f.at[b * IMG:(b + 1) * IMG, 0:DINO]))
        own_f.append(local(siglip.at[b, 0], f.at[b * IMG:(b + 1) * IMG, DINO:FEAT]))
    own_bias = local(bias_in, bias)

    barrier = pltpu.get_barrier_semaphore()
    peers = [(E, eo), (C, co), (Y, yo)]
    peers += [(X, k) for k in (xp, xm, xo)] + [(Z, k) for k in (zp, zm, zo)]
    for axis, to in peers:
        pl.semaphore_signal(
            barrier, inc=1, device_id={axis: to}, device_id_type=pl.DeviceIdType.MESH
        )
    pl.semaphore_wait(barrier, len(peers))

    for copy in own_w:
        copy.wait()
    a1 = remote(ga.at[za, ua], ga.at[za, ua], Y, yo)
    b1p = remote(gb.at[xb, ub], gb.at[xb, ub], Z, zp)
    b1m = remote(gb.at[xb, ub], gb.at[xb, ub], Z, zm)
    far_f = []
    for b in range(2):
        rows = slice(2 * IMG + b * IMG, 2 * IMG + (b + 1) * IMG)
        far_f.append(remote(dino.at[b, 0], f.at[rows, 0:DINO], E, eo))
        far_f.append(remote(siglip.at[b, 0], f.at[rows, DINO:FEAT], E, eo))
    own_hg = []
    for i, image in enumerate((e, eo)):
        for b in range(2):
            own_hg.append(
                local(
                    hg.at[b, pl.ds(pl.multiple_of(image * IMG, IMG), IMG)],
                    lg.at[(2 * i + b) * IMG:(2 * i + b + 1) * IMG],
                )
            )

    a1.wait_recv()
    pair = pl.ds(2 * x, 2)
    a2p = remote(ga.at[za, pair], ga.at[za, pair], X, xp)
    a2m = remote(ga.at[za, pair], ga.at[za, pair], X, xm)
    b1p.wait_recv()
    far = gb.at[xb, y * 4 + zm, :, 0:512]
    b2p = remote(far, far, Z, zp)
    b1m.wait_recv()
    far = gb.at[xb, y * 4 + zp, :, 512:WB]
    b2m = remote(far, far, Z, zm)
    a2p.wait_recv()
    far = ga.at[za, 2 * xm]
    a3p = remote(far, far, X, xp)
    a2m.wait_recv()
    far = ga.at[za, 2 * xp + 1]
    a3m = remote(far, far, X, xm)
    b2p.wait_recv()
    b2m.wait_recv()
    line = gb.at[xb, pl.ds(4 * y, 4)]
    b3 = remote(line, line, Y, yo)
    a3p.wait_recv()
    a3m.wait_recv()
    a4p = remote(ga.at[za], ga.at[za], Z, zp)
    a4m = remote(ga.at[za], ga.at[za], Z, zm)
    b3.wait_recv()
    b4p = remote(gb.at[xb], gb.at[xb], X, xp)
    b4m = remote(gb.at[xb], gb.at[xb], X, xm)
    shared = [remote(ga.at[za], ga.at[za], C, co), remote(gb.at[xb], gb.at[xb], C, co)]

    def transposed(first):
        def step(t, carry):
            cols = pl.ds(pl.multiple_of(t * 128, 128), 128)
            ft[cols, first:first + 512] = f[first:first + 512, cols].T
            return carry
        lax.fori_loop(0, FEAT // 128, step, 0)

    for copy in own_f:
        copy.wait()
    transposed(0)

    a4p.wait_recv()
    blk = zm * 2 + c
    a5p = remote(ga.at[blk, 0:4], ga.at[blk, 0:4], Z, zp)
    shared.append(remote(ga.at[blk], ga.at[blk], C, co))
    a4m.wait_recv()
    blk = zp * 2 + c
    a5m = remote(ga.at[blk, 4:8], ga.at[blk, 4:8], Z, zm)
    shared.append(remote(ga.at[blk], ga.at[blk], C, co))
    b4p.wait_recv()
    blk = xm * 2 + c
    b5p = remote(gb.at[blk, 0:4], gb.at[blk, 0:4], X, xp)
    shared.append(remote(gb.at[blk], gb.at[blk], C, co))
    b4m.wait_recv()
    blk = xp * 2 + c
    b5m = remote(gb.at[blk, 4:8], gb.at[blk, 4:8], X, xm)
    shared.append(remote(gb.at[blk], gb.at[blk], C, co))
    blka, blkb = zo * 2 + c, xo * 2 + c
    a5p.wait_recv()
    shared.append(remote(ga.at[blka, 0:4], ga.at[blka, 0:4], C, co))
    a5m.wait_recv()
    shared.append(remote(ga.at[blka, 4:8], ga.at[blka, 4:8], C, co))
    b5p.wait_recv()
    shared.append(remote(gb.at[blkb, 0:4], gb.at[blkb, 0:4], C, co))
    b5m.wait_recv()
    shared.append(remote(gb.at[blkb, 4:8], gb.at[blkb, 4:8], C, co))
    for copy in shared:
        copy.wait_recv()

    def where_b(g, j):
        return (g // 2) * 2 + j % 2, lax.rem(g, 2) * 4 + j // 2

    def assemble(g, carry):
        rows = pl.ds(pl.multiple_of(g * GROUP, 16), GROUP)
        for j in range(8):
            scr[j * ROWS:(j + 1) * ROWS, 0:WA] = ga[j, g].astype(F32)
        wd[rows, 0:WA] = scr[:, 0:WA].astype(BF16)
        for j in range(8):
            i, k = where_b(g, j)
            scr[j * ROWS:(j + 1) * ROWS, :] = gb[i, k].astype(F32)
        wd[rows, WA:FEAT] = scr[...].astype(BF16)
        return carry

    lax.fori_loop(0, 8, assemble, 0)
    wait_sends()

    bsum[...] = jnp.zeros_like(bsum)
    own_bias.wait()

    def forward(first):
        def tile(start, width):
            cols = pl.ds(start, width)
            pre[:, 0:width] = jnp.dot(
                f[first:first + 512, :], wd[:, cols], preferred_element_type=F32
            )

            def rows_step(r, acc):
                at = pl.ds(pl.multiple_of(r * 32, 32), 32)
                lat = pl.ds(pl.multiple_of(first + r * 32, 32), 32)
                v = pre[at, 0:width] + bias[:, cols]
                cdf = 0.5 + 0.5 * lax.erf(v * 0.7071067811865476)
                pdf = jnp.exp(v * v * -0.5) * 0.3989422804014327
                hid[at, cols] = (v * cdf).astype(BF16)
                grad = (lg[lat, cols].astype(F32) * (cdf + v * pdf)).astype(BF16)
                lg[lat, cols] = grad
                wide = grad.astype(F32)
                return acc + (wide[0:8] + wide[8:16] + wide[16:24] + wide[24:32])

            acc = lax.fori_loop(0, 16, rows_step, jnp.zeros((8, width), F32))
            bsum[:, cols] += jnp.sum(acc, axis=0, keepdims=True)

        def step(t, carry):
            tile(pl.multiple_of(t * 512, 512), 512)
            return carry

        lax.fori_loop(0, 4, step, 0)
        tile(2048, 128)

    def hidden_out(image):
        return [
            local(
                hid.at[b * IMG:(b + 1) * IMG],
                hidden.at[b, pl.ds(pl.multiple_of(image * IMG, IMG), IMG)],
            )
            for b in range(2)
        ]

    def feature_part(first, dst, start, width):
        dst[:, pl.ds(start, width)] = lax.dot_general(
            lg[first:first + 512, :], wd[pl.ds(start, width), :],
            (((1,), (1,)), ((), ())), preferred_element_type=F32,
        ).astype(BF16)

    def feature_half(first, dst, half):
        def step(t, carry):
            feature_part(first, dst, pl.multiple_of(half * 1024 + t * 512, 512), 512)
            return carry
        lax.fori_loop(0, 2, step, 0)
        if half == 1:
            feature_part(first, dst, 2048, 128)

    own_hg[0].wait()
    own_hg[1].wait()
    forward(0)
    outs = hidden_out(e)
    for copy in far_f:
        copy.wait_recv()
    transposed(512)
    own_hg[2].wait()
    own_hg[3].wait()
    for copy in outs:
        copy.wait()
    forward(512)
    outs = hidden_out(eo)
    feature_half(512, fsend, 0)
    back = [remote(fsend.at[:, 0:DINO], frecv.at[:, 0:DINO], E, eo)]
    feature_half(512, fsend, 1)
    back.append(remote(fsend.at[:, DINO:FEAT], frecv.at[:, DINO:FEAT], E, eo))

    bc[c] = bsum[...]
    bias_c = remote(bc.at[c], bc.at[c], C, co)

    def weight_part(g, carry, first, width):
        rows = pl.ds(pl.multiple_of(g * GROUP, 16), GROUP)
        scr[:, 0:width] = jnp.dot(
            ft[rows, :], lg[:, first:first + width], preferred_element_type=F32
        )
        for j in range(8):
            unit = scr[j * ROWS:(j + 1) * ROWS, 0:width].astype(BF16)
            if first == 0:
                ga[j, g] = unit
            else:
                i, k = where_b(g, j)
                gb[i, k] = unit
        return carry

    lax.fori_loop(0, 8, lambda g, s: weight_part(g, s, 0, WA), 0)
    core_a = [remote(ga.at[k * 2 + co], rca.at[k], C, co) for k in (zo, zp, zm, z)]
    lax.fori_loop(0, 8, lambda g, s: weight_part(g, s, WA, WB), 0)
    core_b = [remote(gb.at[k * 2 + co], rcb.at[k], C, co) for k in (xo, xp, xm, x)]

    def add_units(dst, srcs, n):
        def step(k, carry):
            total = dst[k].astype(F32)
            for src in srcs:
                total = total + src[k].astype(F32)
            dst[k] = total.astype(BF16)
            return carry
        lax.fori_loop(0, n, step, 0)

    def hop_one(buf, rc, core, one, two, axis, opp, nxt, prv):
        core[0].wait_recv()
        add_units(buf.at[opp * 2 + c], [rc.at[opp]], 8)
        up = remote(buf.at[opp * 2 + c, 0:4], one.at[0], axis, nxt)
        down = remote(buf.at[opp * 2 + c, 4:8], one.at[1], axis, prv)
        core[1].wait_recv()
        add_units(buf.at[nxt * 2 + c], [rc.at[nxt]], 8)
        near_up = remote(buf.at[nxt * 2 + c, 4:8], two.at[0, 4:8], axis, nxt)
        core[2].wait_recv()
        add_units(buf.at[prv * 2 + c], [rc.at[prv]], 8)
        near_down = remote(buf.at[prv * 2 + c, 0:4], two.at[1, 0:4], axis, prv)
        return up, down, near_up, near_down

    def hop_two(buf, one, two, hops, axis, nxt, prv):
        hops[0].wait_recv()
        add_units(buf.at[nxt * 2 + c, 0:4], [one.at[0]], 4)
        up = remote(buf.at[nxt * 2 + c, 0:4], two.at[0, 0:4], axis, nxt)
        hops[1].wait_recv()
        add_units(buf.at[prv * 2 + c, 4:8], [one.at[1]], 4)
        down = remote(buf.at[prv * 2 + c, 4:8], two.at[1, 4:8], axis, prv)
        return up, down, hops[2], hops[3]

    hops_a = hop_one(ga, rca, core_a, r1a, r2a, Z, zo, zp, zm)
    hops_b = hop_one(gb, rcb, core_b, r1b, r2b, X, xo, xp, xm)

    bias_c.wait_recv()
    bz[z] = bc[0] + bc[1]
    bias_z = [remote(bz.at[z], bz.at[z], Z, k) for k in (zp, zm, zo)]

    core_a[3].wait_recv()
    add_units(ga.at[za], [rca.at[z]], 8)
    core_b[3].wait_recv()
    add_units(gb.at[xb], [rcb.at[x]], 8)
    hops_a = hop_two(ga, r1a, r2a, hops_a, Z, zp, zm)
    hops_b = hop_two(gb, r1b, r2b, hops_b, X, xp, xm)

    own_part = f.at[0:512]
    feature_half(0, own_part, 0)
    feature_half(0, own_part, 1)

    for copy in bias_z:
        copy.wait_recv()
    bx[x] = (bz[0] + bz[1]) + (bz[2] + bz[3])
    bias_x = [remote(bx.at[x], bx.at[x], X, k) for k in (xp, xm, xo)]

    for copy in hops_a:
        copy.wait_recv()
    add_units(ga.at[za], [r2a.at[0], r2a.at[1]], 8)
    t1p = remote(ga.at[za, 2 * xo], q1a.at[0], X, xp)
    t1m = remote(ga.at[za, 2 * xo + 1], q1a.at[1], X, xm)
    t2p = remote(ga.at[za, 2 * xp + 1], q2a.at[0, 1], X, xp)
    t2m = remote(ga.at[za, 2 * xm], q2a.at[1, 0], X, xm)

    for copy in hops_b:
        copy.wait_recv()
    add_units(gb.at[xb], [r2b.at[0], r2b.at[1]], 8)
    far = gb.at[xb, pl.ds(4 * yo, 4)]
    u0 = remote(far, ryb, Y, yo)

    t1p.wait_recv()
    ga[za, 2 * xp] = (ga[za, 2 * xp].astype(F32) + q1a[0].astype(F32)).astype(BF16)
    t3p = remote(ga.at[za, 2 * xp], q2a.at[0, 0], X, xp)
    t1m.wait_recv()
    ga[za, 2 * xm + 1] = (ga[za, 2 * xm + 1].astype(F32) + q1a[1].astype(F32)).astype(BF16)
    t3m = remote(ga.at[za, 2 * xm + 1], q2a.at[1, 1], X, xm)

    u0.wait_recv()
    add_units(gb.at[xb, pl.ds(4 * y, 4)], [ryb], 4)
    near, up, down = y * 4 + zo, y * 4 + zp, y * 4 + zm
    u1p = remote(gb.at[xb, near, :, 0:512], q1b.at[:, 0:512], Z, zp)
    u1m = remote(gb.at[xb, near, :, 512:WB], q1b.at[:, 512:WB], Z, zm)
    u2p = remote(gb.at[xb, up, :, 512:WB], q2b.at[0, :, 512:WB], Z, zp)
    u2m = remote(gb.at[xb, down, :, 0:512], q2b.at[1, :, 0:512], Z, zm)

    for copy in bias_x:
        copy.wait_recv()
    by[y] = (bx[0] + bx[1]) + (bx[2] + bx[3])
    bias_y = remote(by.at[y], by.at[y], Y, yo)

    for copy in (t2p, t2m, t3p, t3m):
        copy.wait_recv()
    add_units(ga.at[za, pair], [q2a.at[0], q2a.at[1]], 2)
    v0 = remote(ga.at[za, 2 * x + yo], rya, Y, yo)

    u1p.wait_recv()
    gb[xb, up, :, 0:512] = (
        gb[xb, up, :, 0:512].astype(F32) + q1b[:, 0:512].astype(F32)
    ).astype(BF16)
    u3p = remote(gb.at[xb, up, :, 0:512], q2b.at[0, :, 0:512], Z, zp)
    u1m.wait_recv()
    gb[xb, down, :, 512:WB] = (
        gb[xb, down, :, 512:WB].astype(F32) + q1b[:, 512:WB].astype(F32)
    ).astype(BF16)
    u3m = remote(gb.at[xb, down, :, 512:WB], q2b.at[1, :, 512:WB], Z, zm)

    for k, copy in enumerate(back):
        copy.wait_recv()

    def last_add(r, carry):
        at = pl.ds(pl.multiple_of(r * 32, 32), 32)
        f[at, :] = (f[at, :].astype(F32) + frecv[at, :].astype(F32)).astype(BF16)
        return carry

    lax.fori_loop(0, 16, last_add, 0)
    for b in range(2):
        outs.append(local(f.at[b * IMG:(b + 1) * IMG, 0:DINO], dino_grad.at[b, 0]))
        outs.append(local(f.at[b * IMG:(b + 1) * IMG, DINO:FEAT], siglip_grad.at[b, 0]))

    v0.wait_recv()
    wout[:, 0:WA] = ga[za, ua].astype(F32) + rya[...].astype(F32)
    for copy in (u2p, u2m, u3p, u3m):
        copy.wait_recv()
    wout[:, WA:FEAT] = (
        gb[xb, ub].astype(F32) + q2b[0].astype(F32) + q2b[1].astype(F32)
    )
    outs.append(local(wout, wgrad))
    bias_y.wait_recv()
    bsum[...] = by[0] + by[1]
    outs.append(local(bsum, bgrad))
    for copy in outs:
        copy.wait()
    wait_sends()


def shards(dino_feats, siglip_feats, proj_weight, proj_bias, hidden_grad):
    vm = pltpu.VMEM
    unit_a, unit_b = (ROWS, WA), (ROWS, WB)
    scratch = [
        vm((8, 8, *unit_a), BF16), vm((8, 8, *unit_b), BF16),
        vm((FEAT, FEAT), BF16), vm((1024, FEAT), BF16), vm((FEAT, 1024), BF16),
        vm((1024, FEAT), BF16), vm((512, FEAT), BF16), vm((512, FEAT), BF16),
        vm((512, FEAT), BF16),
        vm((4, 8, *unit_a), BF16), vm((4, 8, *unit_b), BF16),
        vm((2, 4, *unit_a), BF16), vm((2, 8, *unit_a), BF16),
        vm((2, 4, *unit_b), BF16), vm((2, 8, *unit_b), BF16),
        vm((2, *unit_a), BF16), vm((2, 2, *unit_a), BF16), vm(unit_a, BF16),
        vm(unit_b, BF16), vm((2, *unit_b), BF16), vm((4, *unit_b), BF16),
        vm((GROUP, WB), F32), vm((512, 512), F32), vm((ROWS, FEAT), F32),
        vm((1, FEAT), F32), vm((1, FEAT), F32),
        vm((2, 1, FEAT), F32), vm((4, 1, FEAT), F32), vm((4, 1, FEAT), F32),
        vm((2, 1, FEAT), F32),
        pltpu.SemaphoreType.DMA((COPIES,)), pltpu.SemaphoreType.DMA((COPIES,)),
        pltpu.SemaphoreType.DMA((LOCALS,)),
    ]
    anywhere = pl.BlockSpec(memory_space=pl.ANY)
    hidden, wgrad, bgrad, dino_grad, siglip_grad = pl.pallas_call(
        kernel,
        out_shape=(
            jax.ShapeDtypeStruct(hidden_grad.shape, BF16),
            jax.ShapeDtypeStruct((ROWS, FEAT), F32),
            jax.ShapeDtypeStruct((1, FEAT), F32),
            jax.ShapeDtypeStruct(dino_feats.shape, BF16),
            jax.ShapeDtypeStruct(siglip_feats.shape, BF16),
        ),
        in_specs=[anywhere] * 5,
        out_specs=[anywhere] * 5,
        scratch_shapes=scratch,
        compiler_params=pltpu.CompilerParams(
            collective_id=0, has_side_effects=True, vmem_limit_bytes=62 * 2**20
        ),
        cost_estimate=pl.CostEstimate(
            flops=6 * 1024 * FEAT * FEAT, bytes_accessed=20 * 2**20, transcendentals=4 * 2**20
        ),
    )(dino_feats, siglip_feats, proj_weight, proj_bias.reshape(1, FEAT), hidden_grad)
    return hidden, wgrad, bgrad.reshape(FEAT), dino_grad, siglip_grad


def solution(mesh):
    finer = Mesh(mesh.devices.reshape(mesh.shape["enc"], 4, 2, 4, 2), (E, *FSDP))
    in_specs = (
        P(FSDP, E, None, None), P(FSDP, E, None, None), P(FSDP, E), P(E), P(FSDP, None, E),
    )
    out_specs = (
        P(FSDP, None, E), P(FSDP, E), P(E), P(FSDP, E, None, None), P(FSDP, E, None, None),
    )
    return jax.shard_map(
        shards, mesh=finer, in_specs=in_specs, out_specs=out_specs, check_vma=False
    )
```

```python
import jax
import jax.numpy as jnp
from jax import lax
from jax.experimental import pallas as pl
from jax.experimental.pallas import tpu as pltpu
from jax.sharding import Mesh
from jax.sharding import PartitionSpec as P

E, X, Y, Z, C = "enc", "fsdp_0", "fsdp_1", "fsdp_2", "fsdp_3"
FSDP = (X, Y, Z, C)
DINO = 1024
SIG = 1152
FEAT = 2176
IMG = 256
ROWS = 34
WA = 1024
WB = 1152
GROUP = 8 * ROWS
F32 = jnp.float32
BF16 = jnp.bfloat16
CUT_A = (slice(0, 512), slice(512, WA))
CUT_B = (slice(0, 640), slice(640, WB))
COPIES = 136
LOCALS = 24


def kernel(
    dino, siglip, w, bias_in, hg,
    hidden, wgrad, bgrad, dino_grad, siglip_grad,
    ga, gb, wd, f, ft, lg, hid, fsend, frecv,
    rca, rcb, r1a, r2a, r1b, r2b, q1a, q2a, rya, q1b, q2b, ryb,
    scr, pre, wout, bias, bsum, bc, bz, bx, by, flat_in, flat_out,
    ssem, rsem, lsem,
):
    e, x, y, z, c = (lax.axis_index(n) for n in (E, X, Y, Z, C))
    xp, xm, xo = (lax.rem(x + k, 4) for k in (1, 3, 2))
    zp, zm, zo = (lax.rem(z + k, 4) for k in (1, 3, 2))
    yo, co, eo = 1 - y, 1 - c, 1 - e
    za, ua = z * 2 + c, x * 2 + y
    xb, ub = x * 2 + c, z * 2 + y

    counts = {"remote": 0, "local": 0}
    sends = []

    def remote(src, dst, axis, to):
        i = counts["remote"]
        counts["remote"] += 1
        copy = pltpu.make_async_remote_copy(
            src_ref=src, dst_ref=dst, send_sem=ssem.at[i], recv_sem=rsem.at[i],
            device_id={axis: to}, device_id_type=pl.DeviceIdType.MESH,
        )
        copy.start()
        sends.append(copy)
        return copy

    def local(src, dst):
        i = counts["local"]
        counts["local"] += 1
        copy = pltpu.make_async_copy(src, dst, lsem.at[i])
        copy.start()
        return copy

    def wait_sends():
        for copy in sends:
            copy.wait_send()
        sends.clear()

    own_w = [local(w.at[:, 0:WA], ga.at[za, ua]), local(w.at[:, WA:FEAT], gb.at[xb, ub])]
    own_f = []
    for b in range(2):
        own_f.append(local(dino.at[b, 0], f.at[b * IMG:(b + 1) * IMG, 0:DINO]))
        own_f.append(local(siglip.at[b, 0], f.at[b * IMG:(b + 1) * IMG, DINO:FEAT]))
    own_bias = local(bias_in, flat_in)

    barrier = pltpu.get_barrier_semaphore()
    peers = [(E, eo), (C, co), (Y, yo)]
    peers += [(X, k) for k in (xp, xm, xo)] + [(Z, k) for k in (zp, zm, zo)]
    for axis, to in peers:
        pl.semaphore_signal(
            barrier, inc=1, device_id={axis: to}, device_id_type=pl.DeviceIdType.MESH
        )
    pl.semaphore_wait(barrier, len(peers))

    for copy in own_w:
        copy.wait()
    def across(buf, block, unit):
        return remote(buf.at[block, unit], buf.at[block, unit], Y, yo)

    def near_pair(buf, block, me, axis, nxt, prv):
        pair = buf.at[block, pl.ds(2 * me, 2)]
        return remote(pair, pair, axis, nxt), remote(pair, pair, axis, prv)

    def far_pair(buf, block, hops, axis, nxt, prv):
        hops[0].wait_recv()
        unit = buf.at[block, 2 * prv]
        up = remote(unit, unit, axis, nxt)
        hops[1].wait_recv()
        unit = buf.at[block, 2 * nxt + 1]
        return up, remote(unit, unit, axis, prv)

    def near_block(buf, cols, me, axis, nxt, prv, shared):
        block = buf.at[me * 2 + c, :, :, cols]
        up, down = remote(block, block, axis, nxt), remote(block, block, axis, prv)
        shared.append(remote(block, block, C, co))
        return up, down

    def far_block(buf, cols, hops, axis, nxt, prv, shared):
        hops[0].wait_recv()
        block = buf.at[prv * 2 + c, :, :, cols]
        half = buf.at[prv * 2 + c, 0:4, :, cols]
        up = remote(half, half, axis, nxt)
        shared.append(remote(block, block, C, co))
        hops[1].wait_recv()
        block = buf.at[nxt * 2 + c, :, :, cols]
        half = buf.at[nxt * 2 + c, 4:8, :, cols]
        down = remote(half, half, axis, prv)
        shared.append(remote(block, block, C, co))
        return up, down

    def last_block(buf, cols, hops, opp, shared):
        for k, hop in enumerate(hops):
            hop.wait_recv()
            half = buf.at[opp * 2 + c, 4 * k:4 * k + 4, :, cols]
            shared.append(remote(half, half, C, co))

    def arrived(shared):
        for copy in shared:
            copy.wait_recv()

    shared = ([], [])
    across_a = across(ga, za, ua)
    across_b = across(gb, xb, ub)
    far_f = []
    for b in range(2):
        rows = slice(2 * IMG + b * IMG, 2 * IMG + (b + 1) * IMG)
        far_f.append(remote(dino.at[b, 0], f.at[rows, 0:DINO], E, eo))
        far_f.append(remote(siglip.at[b, 0], f.at[rows, DINO:FEAT], E, eo))
    del sends[-4:]
    own_hg = []
    for i, image in enumerate((e, eo)):
        for b in range(2):
            own_hg.append(
                local(
                    hg.at[b, pl.ds(pl.multiple_of(image * IMG, IMG), IMG)],
                    lg.at[(2 * i + b) * IMG:(2 * i + b + 1) * IMG],
                )
            )

    across_a.wait_recv()
    hops_a = near_pair(ga, za, x, X, xp, xm)
    across_b.wait_recv()
    hops_b = near_pair(gb, xb, z, Z, zp, zm)
    hops_a = far_pair(ga, za, hops_a, X, xp, xm)
    hops_b = far_pair(gb, xb, hops_b, Z, zp, zm)
    for hop in hops_a:
        hop.wait_recv()
    hops_a = near_block(ga, CUT_A[0], z, Z, zp, zm, shared[0])
    for hop in hops_b:
        hop.wait_recv()
    hops_b = near_block(gb, CUT_B[0], x, X, xp, xm, shared[0])

    def transposed(first, count):
        def step(t, carry):
            cols = pl.ds(pl.multiple_of(t * 128, 128), 128)
            ft[cols, first:first + count] = f[first:first + count, cols].T
            return carry
        lax.fori_loop(0, FEAT // 128, step, 0)

    for copy in own_f:
        copy.wait()
    transposed(0, 512)

    hops_a = far_block(ga, CUT_A[0], hops_a, Z, zp, zm, shared[0])
    then_a = near_block(ga, CUT_A[1], z, Z, zp, zm, shared[1])
    hops_b = far_block(gb, CUT_B[0], hops_b, X, xp, xm, shared[0])
    then_b = near_block(gb, CUT_B[1], x, X, xp, xm, shared[1])
    last_block(ga, CUT_A[0], hops_a, zo, shared[0])
    last_block(gb, CUT_B[0], hops_b, xo, shared[0])
    arrived(shared[0])

    def where_b(g, j):
        return (g // 2) * 2 + j % 2, (j // 2) * 2 + lax.rem(g, 2)

    def assembled(n):
        def step(g, carry):
            rows = pl.ds(pl.multiple_of(g * GROUP, 16), GROUP)
            cols = CUT_A[n]
            for j in range(8):
                scr[j * ROWS:(j + 1) * ROWS, 0:512] = ga[j, g, :, cols].astype(F32)
            wd[rows, cols] = scr[:, 0:512].astype(BF16)
            cols = CUT_B[n]
            width = cols.stop - cols.start
            for j in range(8):
                i, k = where_b(g, j)
                scr[j * ROWS:(j + 1) * ROWS, 0:width] = gb[i, k, :, cols].astype(F32)
            wd[rows, WA + cols.start:WA + cols.stop] = scr[:, 0:width].astype(BF16)
            return carry
        lax.fori_loop(0, 8, step, 0)

    assembled(0)

    bsum[...] = jnp.zeros_like(bsum)
    own_bias.wait()
    bias[...] = flat_in[...].reshape(1, FEAT)

    def forward(n, first, count):
        def tile(start, width):
            cols = pl.ds(start, width)
            pre[0:count, 0:width] = jnp.dot(
                f[first:first + count, :], wd[:, cols], preferred_element_type=F32
            )

            def rows_step(r, acc):
                at = pl.ds(pl.multiple_of(r * 32, 32), 32)
                lat = pl.ds(pl.multiple_of(first + r * 32, 32), 32)
                v = pre[at, 0:width] + bias[:, cols]
                cdf = 0.5 + 0.5 * lax.erf(v * 0.7071067811865476)
                pdf = jnp.exp(v * v * -0.5) * 0.3989422804014327
                hid[lat, cols] = (v * cdf).astype(BF16)
                grad = (lg[lat, cols].astype(F32) * (cdf + v * pdf)).astype(BF16)
                lg[lat, cols] = grad
                wide = grad.astype(F32)
                return acc + (wide[0:8] + wide[8:16] + wide[16:24] + wide[24:32])

            acc = lax.fori_loop(0, count // 32, rows_step, jnp.zeros((8, width), F32))
            bsum[:, cols] += jnp.sum(acc, axis=0, keepdims=True)

        tile(CUT_A[n].start, 512)
        tile(WA + CUT_B[n].start, CUT_B[n].stop - CUT_B[n].start)

    def hidden_out(k):
        image = e if k < 2 else eo
        return local(
            hid.at[k * IMG:(k + 1) * IMG],
            hidden.at[k % 2, pl.ds(pl.multiple_of(image * IMG, IMG), IMG)],
        )

    def feature_part(first, count, dst, start, width):
        dst[:, pl.ds(start, width)] = lax.dot_general(
            lg[first:first + count, :], wd[pl.ds(start, width), :],
            (((1,), (1,)), ((), ())), preferred_element_type=F32,
        ).astype(BF16)

    def feature_grad(first, count, dst):
        def step(t, carry):
            feature_part(first, count, dst, pl.multiple_of(t * 512, 512), 512)
            return carry
        lax.fori_loop(0, 4, step, 0)
        feature_part(first, count, dst, 2048, 128)

    def give_back(k):
        rows = slice(k * IMG, (k + 1) * IMG)
        feature_grad((2 + k) * IMG, IMG, fsend.at[rows])
        back.append(remote(fsend.at[rows], frecv.at[rows], E, eo))

    outs, back = [], []
    own_hg[0].wait()
    own_hg[1].wait()
    forward(0, 0, 2 * IMG)
    hops_a = far_block(ga, CUT_A[1], then_a, Z, zp, zm, shared[1])
    hops_b = far_block(gb, CUT_B[1], then_b, X, xp, xm, shared[1])
    far_f[0].wait_recv()
    far_f[1].wait_recv()
    own_hg[2].wait()
    forward(0, 2 * IMG, IMG)
    last_block(ga, CUT_A[1], hops_a, zo, shared[1])
    last_block(gb, CUT_B[1], hops_b, xo, shared[1])
    transposed(2 * IMG, IMG)
    arrived(shared[1])
    gathered = list(sends)
    sends.clear()
    assembled(1)
    forward(1, 2 * IMG, IMG)
    outs.append(hidden_out(2))
    give_back(0)
    forward(1, 0, 2 * IMG)
    outs.append(hidden_out(0))
    outs.append(hidden_out(1))
    far_f[2].wait_recv()
    far_f[3].wait_recv()
    own_hg[3].wait()
    forward(0, 3 * IMG, IMG)
    forward(1, 3 * IMG, IMG)
    outs.append(hidden_out(3))
    transposed(3 * IMG, IMG)
    for copy in gathered:
        copy.wait_send()
    sends.extend(far_f)

    bc[c] = bsum[...]
    bias_c = remote(bc.at[c], bc.at[c], C, co)

    def weight_part(buf, cols):
        width = cols.stop - cols.start
        at = slice(cols.start + (WA if buf is gb else 0), cols.stop + (WA if buf is gb else 0))

        def step(g, carry):
            rows = pl.ds(pl.multiple_of(g * GROUP, 16), GROUP)
            scr[:, 0:width] = jnp.dot(ft[rows, :], lg[:, at], preferred_element_type=F32)
            for j in range(8):
                i, k = where_b(g, j) if buf is gb else (j, g)
                buf[i, k, :, cols] = scr[j * ROWS:(j + 1) * ROWS, 0:width].astype(BF16)
            return carry

        lax.fori_loop(0, 8, step, 0)

    def core_part(buf, rc, cols, order):
        weight_part(buf, cols)
        return [
            remote(buf.at[k * 2 + co, :, :, cols], rc.at[k, :, :, cols], C, co) for k in order
        ]

    def add_units(dst, srcs, n):
        def step(k, carry):
            total = dst[k].astype(F32)
            for src in srcs:
                total = total + src[k].astype(F32)
            dst[k] = total.astype(BF16)
            return carry
        lax.fori_loop(0, n, step, 0)

    def hop_one(buf, rc, core, one, two, cols, axis, opp, nxt, prv):
        def block(k):
            return buf.at[k * 2 + c, :, :, cols]

        def part(ref, *at):
            return ref.at[(*at, slice(None), cols)]

        low, high = slice(0, 4), slice(4, 8)
        core[0].wait_recv()
        add_units(block(opp), [rc.at[opp, :, :, cols]], 8)
        up = remote(part(buf, opp * 2 + c, low), part(one, 0, slice(None)), axis, nxt)
        down = remote(part(buf, opp * 2 + c, high), part(one, 1, slice(None)), axis, prv)
        core[1].wait_recv()
        add_units(block(nxt), [rc.at[nxt, :, :, cols]], 8)
        near_up = remote(part(buf, nxt * 2 + c, high), part(two, 0, high), axis, nxt)
        core[2].wait_recv()
        add_units(block(prv), [rc.at[prv, :, :, cols]], 8)
        near_down = remote(part(buf, prv * 2 + c, low), part(two, 1, low), axis, prv)
        return up, down, near_up, near_down

    def hop_two(buf, one, two, cols, hops, axis, nxt, prv):
        hops[0].wait_recv()
        half = buf.at[nxt * 2 + c, 0:4, :, cols]
        add_units(half, [one.at[0, :, :, cols]], 4)
        up = remote(half, two.at[0, 0:4, :, cols], axis, nxt)
        hops[1].wait_recv()
        half = buf.at[prv * 2 + c, 4:8, :, cols]
        add_units(half, [one.at[1, :, :, cols]], 4)
        down = remote(half, two.at[1, 4:8, :, cols], axis, prv)
        return up, down, hops[2], hops[3]

    def own_block(buf, rc, core, cols, me):
        core[3].wait_recv()
        add_units(buf.at[me * 2 + c, :, :, cols], [rc.at[me, :, :, cols]], 8)

    def hop_last(buf, two, cols, hops, me):
        for copy in hops:
            copy.wait_recv()
        add_units(
            buf.at[me * 2 + c, :, :, cols],
            [two.at[0, :, :, cols], two.at[1, :, :, cols]], 8,
        )

    order_a, order_b = (zo, zp, zm, z), (xo, xp, xm, x)
    along_a, along_b = (Z, zo, zp, zm), (X, xo, xp, xm)
    core_a0 = core_part(ga, rca, CUT_A[0], order_a)
    core_b0 = core_part(gb, rcb, CUT_B[0], order_b)
    hops_a0 = hop_one(ga, rca, core_a0, r1a, r2a, CUT_A[0], *along_a)
    core_a1 = core_part(ga, rca, CUT_A[1], order_a)
    hops_b0 = hop_one(gb, rcb, core_b0, r1b, r2b, CUT_B[0], *along_b)
    give_back(1)
    core_b1 = core_part(gb, rcb, CUT_B[1], order_b)
    hops_a0 = hop_two(ga, r1a, r2a, CUT_A[0], hops_a0, Z, zp, zm)
    hops_a1 = hop_one(ga, rca, core_a1, r1a, r2a, CUT_A[1], *along_a)
    hops_b0 = hop_two(gb, r1b, r2b, CUT_B[0], hops_b0, X, xp, xm)
    hops_b1 = hop_one(gb, rcb, core_b1, r1b, r2b, CUT_B[1], *along_b)

    def pair_one(buf, block, q1, q2, cols, axis, opp, nxt, prv):
        def unit(k):
            return buf.at[block, k, :, cols]

        up = remote(unit(2 * opp), q1.at[0, :, cols], axis, nxt)
        down = remote(unit(2 * opp + 1), q1.at[1, :, cols], axis, prv)
        near_up = remote(unit(2 * nxt + 1), q2.at[0, 1, :, cols], axis, nxt)
        near_down = remote(unit(2 * prv), q2.at[1, 0, :, cols], axis, prv)
        return up, down, near_up, near_down

    def pair_two(buf, block, q1, q2, cols, hops, axis, nxt, prv):
        def add(k, src):
            total = buf[block, k, :, cols].astype(F32) + src[:, cols].astype(F32)
            buf[block, k, :, cols] = total.astype(BF16)
            return buf.at[block, k, :, cols]

        hops[0].wait_recv()
        up = remote(add(2 * nxt, q1.at[0]), q2.at[0, 0, :, cols], axis, nxt)
        hops[1].wait_recv()
        down = remote(add(2 * prv + 1, q1.at[1]), q2.at[1, 1, :, cols], axis, prv)
        return up, down, hops[2], hops[3]

    def pair_last(buf, block, q2, cols, hops, me):
        for copy in hops:
            copy.wait_recv()
        add_units(
            buf.at[block, pl.ds(2 * me, 2), :, cols],
            [q2.at[0, :, :, cols], q2.at[1, :, :, cols]], 2,
        )

    def returned(k):
        back[k].wait_recv()

        def step(r, carry):
            at = pl.ds(pl.multiple_of(k * IMG + r * 32, 32), 32)
            f[at, :] = (f[at, :].astype(F32) + frecv[at, :].astype(F32)).astype(BF16)
            return carry

        lax.fori_loop(0, 8, step, 0)
        outs.append(local(f.at[k * IMG:(k + 1) * IMG, 0:DINO], dino_grad.at[k, 0]))
        outs.append(local(f.at[k * IMG:(k + 1) * IMG, DINO:FEAT], siglip_grad.at[k, 0]))

    bias_c.wait_recv()
    bz[z] = bc[0] + bc[1]
    bias_z = [remote(bz.at[z], bz.at[z], Z, k) for k in (zp, zm, zo)]

    pair_a, pair_b = (za, q1a, q2a), (xb, q1b, q2b)
    own_block(ga, rca, core_a0, CUT_A[0], z)
    hop_last(ga, r2a, CUT_A[0], hops_a0, z)
    hops_a0 = pair_one(ga, *pair_a, CUT_A[0], X, xo, xp, xm)
    own_block(gb, rcb, core_b0, CUT_B[0], x)
    hop_last(gb, r2b, CUT_B[0], hops_b0, x)
    hops_b0 = pair_one(gb, *pair_b, CUT_B[0], Z, zo, zp, zm)
    hops_a1 = hop_two(ga, r1a, r2a, CUT_A[1], hops_a1, Z, zp, zm)
    hops_b1 = hop_two(gb, r1b, r2b, CUT_B[1], hops_b1, X, xp, xm)
    own_block(ga, rca, core_a1, CUT_A[1], z)
    own_block(gb, rcb, core_b1, CUT_B[1], x)
    hops_a0 = pair_two(ga, *pair_a, CUT_A[0], hops_a0, X, xp, xm)
    hops_b0 = pair_two(gb, *pair_b, CUT_B[0], hops_b0, Z, zp, zm)

    feature_grad(0, 2 * IMG, f.at[0:2 * IMG])

    hop_last(ga, r2a, CUT_A[1], hops_a1, z)
    hops_a1 = pair_one(ga, *pair_a, CUT_A[1], X, xo, xp, xm)
    hop_last(gb, r2b, CUT_B[1], hops_b1, x)
    hops_b1 = pair_one(gb, *pair_b, CUT_B[1], Z, zo, zp, zm)

    for copy in bias_z:
        copy.wait_recv()
    bx[x] = (bz[0] + bz[1]) + (bz[2] + bz[3])
    bias_x = [remote(bx.at[x], bx.at[x], X, k) for k in (xp, xm, xo)]

    returned(0)
    pair_last(ga, za, q2a, CUT_A[0], hops_a0, x)
    pair_last(gb, xb, q2b, CUT_B[0], hops_b0, z)
    hops_a1 = pair_two(ga, *pair_a, CUT_A[1], hops_a1, X, xp, xm)
    hops_b1 = pair_two(gb, *pair_b, CUT_B[1], hops_b1, Z, zp, zm)
    for copy in bias_x:
        copy.wait_recv()
    by[y] = (bx[0] + bx[1]) + (bx[2] + bx[3])
    bias_y = remote(by.at[y], by.at[y], Y, yo)
    pair_last(ga, za, q2a, CUT_A[1], hops_a1, x)
    end_a = remote(ga.at[za, 2 * x + yo], rya, Y, yo)
    pair_last(gb, xb, q2b, CUT_B[1], hops_b1, z)
    end_b = remote(gb.at[xb, 2 * z + yo], ryb, Y, yo)
    returned(1)

    end_a.wait_recv()
    wout[:, 0:WA] = ga[za, ua].astype(F32) + rya[...].astype(F32)
    end_b.wait_recv()
    wout[:, WA:FEAT] = gb[xb, ub].astype(F32) + ryb[...].astype(F32)
    outs.append(local(wout, wgrad))
    bias_y.wait_recv()
    flat_out[...] = (by[0] + by[1]).reshape(FEAT)
    outs.append(local(flat_out, bgrad))
    for copy in outs:
        copy.wait()
    wait_sends()


def handed_on(*refs):
    srcs, dsts, held, sem = refs[:5], refs[5:10], refs[10:15], refs[15]
    pieces = [(0, (b, slice(r * 128, (r + 1) * 128))) for b in range(2) for r in range(4)]
    pieces += [(k, b) for k in (3, 4) for b in range(2)] + [(1, ...), (2, ...)]

    def part(ref, at):
        return ref if at is ... else ref.at[at]

    ins, outs = [], []
    for n, (k, at) in enumerate(pieces):
        ins.append(pltpu.make_async_copy(part(srcs[k], at), part(held[k], at), sem.at[0, n]))
        outs.append(pltpu.make_async_copy(part(held[k], at), part(dsts[k], at), sem.at[1, n]))
    for copy in ins:
        copy.start()
    for fetched, copy in zip(ins, outs):
        fetched.wait()
        copy.start()
    for copy in outs:
        copy.wait()


def shards(dino_feats, siglip_feats, proj_weight, proj_bias, hidden_grad):
    vm = pltpu.VMEM
    unit_a, unit_b = (ROWS, WA), (ROWS, WB)
    scratch = [
        vm((8, 8, *unit_a), BF16), vm((8, 8, *unit_b), BF16),
        vm((FEAT, FEAT), BF16), vm((1024, FEAT), BF16), vm((FEAT, 1024), BF16),
        vm((1024, FEAT), BF16), vm((1024, FEAT), BF16), vm((512, FEAT), BF16),
        vm((512, FEAT), BF16),
        vm((4, 8, *unit_a), BF16), vm((4, 8, *unit_b), BF16),
        vm((2, 4, *unit_a), BF16), vm((2, 8, *unit_a), BF16),
        vm((2, 4, *unit_b), BF16), vm((2, 8, *unit_b), BF16),
        vm((2, *unit_a), BF16), vm((2, 2, *unit_a), BF16), vm(unit_a, BF16),
        vm((2, *unit_b), BF16), vm((2, 2, *unit_b), BF16), vm(unit_b, BF16),
        vm((GROUP, WB), F32), vm((512, 640), F32), vm((ROWS, FEAT), F32),
        vm((1, FEAT), F32), vm((1, FEAT), F32),
        vm((2, 1, FEAT), F32), vm((4, 1, FEAT), F32), vm((4, 1, FEAT), F32),
        vm((2, 1, FEAT), F32), vm((FEAT,), F32), vm((FEAT,), F32),
        pltpu.SemaphoreType.DMA((COPIES,)), pltpu.SemaphoreType.DMA((COPIES,)),
        pltpu.SemaphoreType.DMA((LOCALS,)),
    ]
    anywhere = pl.BlockSpec(memory_space=pl.ANY)
    results = pl.pallas_call(
        kernel,
        out_shape=(
            jax.ShapeDtypeStruct(hidden_grad.shape, BF16),
            jax.ShapeDtypeStruct((ROWS, FEAT), F32),
            jax.ShapeDtypeStruct((FEAT,), F32),
            jax.ShapeDtypeStruct(dino_feats.shape, BF16),
            jax.ShapeDtypeStruct(siglip_feats.shape, BF16),
        ),
        in_specs=[anywhere] * 5,
        out_specs=[anywhere] * 5,
        scratch_shapes=scratch,
        compiler_params=pltpu.CompilerParams(
            collective_id=0, has_side_effects=True, vmem_limit_bytes=62 * 2**20
        ),
        cost_estimate=pl.CostEstimate(
            flops=6 * 1024 * FEAT * FEAT, bytes_accessed=20 * 2**20, transcendentals=4 * 2**20
        ),
    )(dino_feats, siglip_feats, proj_weight, proj_bias, hidden_grad)
    return pl.pallas_call(
        handed_on,
        out_shape=tuple(jax.ShapeDtypeStruct(r.shape, r.dtype) for r in results),
        in_specs=[anywhere] * 5,
        out_specs=[anywhere] * 5,
        scratch_shapes=[vm(r.shape, r.dtype) for r in results] + [pltpu.SemaphoreType.DMA((2, 14))],
        cost_estimate=pl.CostEstimate(flops=0, bytes_accessed=14 * 2**20, transcendentals=0),
    )(*results)


def solution(mesh):
    finer = Mesh(mesh.devices.reshape(mesh.shape["enc"], 4, 2, 4, 2), (E, *FSDP))
    in_specs = (
        P(FSDP, E, None, None), P(FSDP, E, None, None), P(FSDP, E), P(E), P(FSDP, None, E),
    )
    out_specs = (
        P(FSDP, None, E), P(FSDP, E), P(E), P(FSDP, E, None, None), P(FSDP, E, None, None),
    )
    return jax.shard_map(
        shards, mesh=finer, in_specs=in_specs, out_specs=out_specs, check_vma=False
    )
```

```python
import jax
import jax.numpy as jnp
from jax import lax
from jax.experimental import pallas as pl
from jax.experimental.pallas import tpu as pltpu
from jax.sharding import Mesh
from jax.sharding import PartitionSpec as P

E, X, Y, Z, C = "enc", "fsdp_0", "fsdp_1", "fsdp_2", "fsdp_3"
FSDP = (X, Y, Z, C)
DINO = 1024
SIG = 1152
FEAT = 2176
IMG = 256
ROWS = 34
WA = 1024
WB = 1152
GROUP = 8 * ROWS
F32 = jnp.float32
BF16 = jnp.bfloat16
CUT_A = (slice(0, 512), slice(512, WA))
CUT_B = (slice(0, 640), slice(640, WB))
COPIES = 136
LOCALS = 24


def kernel(
    dino, siglip, w, bias_in, hg,
    hidden, wgrad, bgrad, dino_grad, siglip_grad,
    ga, gb, wd, f, ft, lg, hid, fsend, frecv,
    rca, rcb, r1a, r2a, r1b, r2b, q1a, q2a, rya, q1b, q2b, ryb,
    scr, pre, pre_next, wout, bias, bsum, bc, bz, bx, by, flat_in, flat_out,
    ssem, rsem, lsem,
):
    e, x, y, z, c = (lax.axis_index(n) for n in (E, X, Y, Z, C))
    xp, xm, xo = (lax.rem(x + k, 4) for k in (1, 3, 2))
    zp, zm, zo = (lax.rem(z + k, 4) for k in (1, 3, 2))
    yo, co, eo = 1 - y, 1 - c, 1 - e
    za, ua = z * 2 + c, x * 2 + y
    xb, ub = x * 2 + c, z * 2 + y

    counts = {"remote": 0, "local": 0}
    sends = []

    def remote(src, dst, axis, to):
        i = counts["remote"]
        counts["remote"] += 1
        copy = pltpu.make_async_remote_copy(
            src_ref=src, dst_ref=dst, send_sem=ssem.at[i], recv_sem=rsem.at[i],
            device_id={axis: to}, device_id_type=pl.DeviceIdType.MESH,
        )
        copy.start()
        sends.append(copy)
        return copy

    def local(src, dst):
        i = counts["local"]
        counts["local"] += 1
        copy = pltpu.make_async_copy(src, dst, lsem.at[i])
        copy.start()
        return copy

    def wait_sends():
        for copy in sends:
            copy.wait_send()
        sends.clear()

    own_w = [local(w.at[:, 0:WA], ga.at[za, ua]), local(w.at[:, WA:FEAT], gb.at[xb, ub])]
    own_f = []
    for b in range(2):
        own_f.append(local(dino.at[b, 0], f.at[b * IMG:(b + 1) * IMG, 0:DINO]))
        own_f.append(local(siglip.at[b, 0], f.at[b * IMG:(b + 1) * IMG, DINO:FEAT]))
    own_bias = local(bias_in, flat_in)

    barrier = pltpu.get_barrier_semaphore()
    peers = [(E, eo), (C, co), (Y, yo)]
    peers += [(X, k) for k in (xp, xm, xo)] + [(Z, k) for k in (zp, zm, zo)]
    for axis, to in peers:
        pl.semaphore_signal(
            barrier, inc=1, device_id={axis: to}, device_id_type=pl.DeviceIdType.MESH
        )
    pl.semaphore_wait(barrier, len(peers))

    for copy in own_w:
        copy.wait()
    def across(buf, block, unit):
        return remote(buf.at[block, unit], buf.at[block, unit], Y, yo)

    def near_pair(buf, block, me, axis, nxt, prv):
        pair = buf.at[block, pl.ds(2 * me, 2)]
        return remote(pair, pair, axis, nxt), remote(pair, pair, axis, prv)

    def far_pair(buf, block, hops, axis, nxt, prv):
        hops[0].wait_recv()
        unit = buf.at[block, 2 * prv]
        up = remote(unit, unit, axis, nxt)
        hops[1].wait_recv()
        unit = buf.at[block, 2 * nxt + 1]
        return up, remote(unit, unit, axis, prv)

    def near_block(buf, cols, me, axis, nxt, prv, shared):
        block = buf.at[me * 2 + c, :, :, cols]
        up, down = remote(block, block, axis, nxt), remote(block, block, axis, prv)
        shared.append(remote(block, block, C, co))
        return up, down

    def far_block(buf, cols, hops, axis, nxt, prv, shared):
        hops[0].wait_recv()
        block = buf.at[prv * 2 + c, :, :, cols]
        half = buf.at[prv * 2 + c, 0:4, :, cols]
        up = remote(half, half, axis, nxt)
        shared.append(remote(block, block, C, co))
        hops[1].wait_recv()
        block = buf.at[nxt * 2 + c, :, :, cols]
        half = buf.at[nxt * 2 + c, 4:8, :, cols]
        down = remote(half, half, axis, prv)
        shared.append(remote(block, block, C, co))
        return up, down

    def last_block(buf, cols, hops, opp, shared):
        for k, hop in enumerate(hops):
            hop.wait_recv()
            half = buf.at[opp * 2 + c, 4 * k:4 * k + 4, :, cols]
            shared.append(remote(half, half, C, co))

    def arrived(shared):
        for copy in shared:
            copy.wait_recv()

    shared = ([], [])
    across_a = across(ga, za, ua)
    across_b = across(gb, xb, ub)
    far_f = []
    for b in range(2):
        rows = slice(2 * IMG + b * IMG, 2 * IMG + (b + 1) * IMG)
        far_f.append(remote(dino.at[b, 0], f.at[rows, 0:DINO], E, eo))
        far_f.append(remote(siglip.at[b, 0], f.at[rows, DINO:FEAT], E, eo))
    del sends[-4:]
    own_hg = []
    for i, image in enumerate((e, eo)):
        for b in range(2):
            own_hg.append(
                local(
                    hg.at[b, pl.ds(pl.multiple_of(image * IMG, IMG), IMG)],
                    lg.at[(2 * i + b) * IMG:(2 * i + b + 1) * IMG],
                )
            )

    across_a.wait_recv()
    hops_a = near_pair(ga, za, x, X, xp, xm)
    across_b.wait_recv()
    hops_b = near_pair(gb, xb, z, Z, zp, zm)
    hops_a = far_pair(ga, za, hops_a, X, xp, xm)
    hops_b = far_pair(gb, xb, hops_b, Z, zp, zm)
    for hop in hops_a:
        hop.wait_recv()
    hops_a = near_block(ga, CUT_A[0], z, Z, zp, zm, shared[0])
    for hop in hops_b:
        hop.wait_recv()
    hops_b = near_block(gb, CUT_B[0], x, X, xp, xm, shared[0])

    def transposed(first, count):
        def step(t, carry):
            cols = pl.ds(pl.multiple_of(t * 128, 128), 128)
            ft[cols, first:first + count] = f[first:first + count, cols].T
            return carry
        lax.fori_loop(0, FEAT // 128, step, 0)

    for copy in own_f:
        copy.wait()
    transposed(0, 512)

    hops_a = far_block(ga, CUT_A[0], hops_a, Z, zp, zm, shared[0])
    then_a = near_block(ga, CUT_A[1], z, Z, zp, zm, shared[1])
    hops_b = far_block(gb, CUT_B[0], hops_b, X, xp, xm, shared[0])
    then_b = near_block(gb, CUT_B[1], x, X, xp, xm, shared[1])
    last_block(ga, CUT_A[0], hops_a, zo, shared[0])
    last_block(gb, CUT_B[0], hops_b, xo, shared[0])
    arrived(shared[0])

    def where_b(g, j):
        return (g // 2) * 2 + j % 2, (j // 2) * 2 + lax.rem(g, 2)

    def assembled(n):
        def step(g, carry):
            rows = pl.ds(pl.multiple_of(g * GROUP, 16), GROUP)
            cols = CUT_A[n]
            for j in range(8):
                scr[j * ROWS:(j + 1) * ROWS, 0:512] = ga[j, g, :, cols].astype(F32)
            wd[rows, cols] = scr[:, 0:512].astype(BF16)
            cols = CUT_B[n]
            width = cols.stop - cols.start
            for j in range(8):
                i, k = where_b(g, j)
                scr[j * ROWS:(j + 1) * ROWS, 0:width] = gb[i, k, :, cols].astype(F32)
            wd[rows, WA + cols.start:WA + cols.stop] = scr[:, 0:width].astype(BF16)
            return carry
        lax.fori_loop(0, 8, step, 0)

    assembled(0)

    bsum[...] = jnp.zeros_like(bsum)
    own_bias.wait()
    bias[...] = flat_in[...].reshape(1, FEAT)

    def forward(n, first, count):
        tiles = []
        for start, stop in (
            (CUT_A[n].start, CUT_A[n].stop), (WA + CUT_B[n].start, WA + CUT_B[n].stop)
        ):
            tiles += [slice(k, min(k + 256, stop)) for k in range(start, stop, 256)]
        slots = (pre, pre_next)

        def product(k):
            cols = tiles[k]
            slots[k % 2][0:count, 0:cols.stop - cols.start] = jnp.dot(
                f[first:first + count, :], wd[:, cols], preferred_element_type=F32
            )

        def activation(k):
            cols = tiles[k]
            width = cols.stop - cols.start
            slot = slots[k % 2]
            shift = bias[:, cols]
            acc = jnp.zeros((8, width), F32)
            for r in range(count // 16):
                at = slice(r * 16, (r + 1) * 16)
                lat = slice(first + r * 16, first + (r + 1) * 16)
                v = slot[at, 0:width] + shift
                cdf = 0.5 + 0.5 * lax.erf(v * 0.7071067811865476)
                pdf = jnp.exp(v * v * -0.5) * 0.3989422804014327
                hid[lat, cols] = (v * cdf).astype(BF16)
                grad = (lg[lat, cols].astype(F32) * (cdf + v * pdf)).astype(BF16)
                lg[lat, cols] = grad
                wide = grad.astype(F32)
                acc = acc + (wide[0:8] + wide[8:16])
            bsum[:, cols] += jnp.sum(acc, axis=0, keepdims=True)

        product(0)
        for k in range(len(tiles)):
            if k + 1 < len(tiles):
                product(k + 1)
            activation(k)

    def hidden_out(k):
        image = e if k < 2 else eo
        return local(
            hid.at[k * IMG:(k + 1) * IMG],
            hidden.at[k % 2, pl.ds(pl.multiple_of(image * IMG, IMG), IMG)],
        )

    def feature_part(first, count, dst, start, width):
        dst[:, pl.ds(start, width)] = lax.dot_general(
            lg[first:first + count, :], wd[pl.ds(start, width), :],
            (((1,), (1,)), ((), ())), preferred_element_type=F32,
        ).astype(BF16)

    def feature_grad(first, count, dst):
        def step(t, carry):
            feature_part(first, count, dst, pl.multiple_of(t * 512, 512), 512)
            return carry
        lax.fori_loop(0, 4, step, 0)
        feature_part(first, count, dst, 2048, 128)

    def give_back(k):
        rows = slice(k * IMG, (k + 1) * IMG)
        feature_grad((2 + k) * IMG, IMG, fsend.at[rows])
        back.append(remote(fsend.at[rows], frecv.at[rows], E, eo))

    outs, back = [], []
    own_hg[0].wait()
    own_hg[1].wait()
    forward(0, 0, 2 * IMG)
    hops_a = far_block(ga, CUT_A[1], then_a, Z, zp, zm, shared[1])
    hops_b = far_block(gb, CUT_B[1], then_b, X, xp, xm, shared[1])
    far_f[0].wait_recv()
    far_f[1].wait_recv()
    own_hg[2].wait()
    forward(0, 2 * IMG, IMG)
    last_block(ga, CUT_A[1], hops_a, zo, shared[1])
    last_block(gb, CUT_B[1], hops_b, xo, shared[1])
    transposed(2 * IMG, IMG)
    arrived(shared[1])
    gathered = list(sends)
    sends.clear()
    assembled(1)
    forward(1, 2 * IMG, IMG)
    outs.append(hidden_out(2))
    give_back(0)
    forward(1, 0, 2 * IMG)
    outs.append(hidden_out(0))
    outs.append(hidden_out(1))
    far_f[2].wait_recv()
    far_f[3].wait_recv()
    own_hg[3].wait()
    forward(0, 3 * IMG, IMG)
    forward(1, 3 * IMG, IMG)
    outs.append(hidden_out(3))
    transposed(3 * IMG, IMG)
    for copy in gathered:
        copy.wait_send()
    sends.extend(far_f)

    bc[c] = bsum[...]
    bias_c = remote(bc.at[c], bc.at[c], C, co)

    def weight_part(buf, cols):
        width = cols.stop - cols.start
        at = slice(cols.start + (WA if buf is gb else 0), cols.stop + (WA if buf is gb else 0))

        def step(g, carry):
            rows = pl.ds(pl.multiple_of(g * GROUP, 16), GROUP)
            scr[:, 0:width] = jnp.dot(ft[rows, :], lg[:, at], preferred_element_type=F32)
            for j in range(8):
                i, k = where_b(g, j) if buf is gb else (j, g)
                buf[i, k, :, cols] = scr[j * ROWS:(j + 1) * ROWS, 0:width].astype(BF16)
            return carry

        lax.fori_loop(0, 8, step, 0)

    def core_part(buf, rc, cols, order):
        weight_part(buf, cols)
        return [
            remote(buf.at[k * 2 + co, :, :, cols], rc.at[k, :, :, cols], C, co) for k in order
        ]

    def add_units(dst, srcs, n):
        def step(k, carry):
            total = dst[k].astype(F32)
            for src in srcs:
                total = total + src[k].astype(F32)
            dst[k] = total.astype(BF16)
            return carry
        lax.fori_loop(0, n, step, 0)

    def hop_one(buf, rc, core, one, two, cols, axis, opp, nxt, prv):
        def block(k):
            return buf.at[k * 2 + c, :, :, cols]

        def part(ref, *at):
            return ref.at[(*at, slice(None), cols)]

        low, high = slice(0, 4), slice(4, 8)
        core[0].wait_recv()
        add_units(block(opp), [rc.at[opp, :, :, cols]], 8)
        up = remote(part(buf, opp * 2 + c, low), part(one, 0, slice(None)), axis, nxt)
        down = remote(part(buf, opp * 2 + c, high), part(one, 1, slice(None)), axis, prv)
        core[1].wait_recv()
        add_units(block(nxt), [rc.at[nxt, :, :, cols]], 8)
        near_up = remote(part(buf, nxt * 2 + c, high), part(two, 0, high), axis, nxt)
        core[2].wait_recv()
        add_units(block(prv), [rc.at[prv, :, :, cols]], 8)
        near_down = remote(part(buf, prv * 2 + c, low), part(two, 1, low), axis, prv)
        return up, down, near_up, near_down

    def hop_two(buf, one, two, cols, hops, axis, nxt, prv):
        hops[0].wait_recv()
        half = buf.at[nxt * 2 + c, 0:4, :, cols]
        add_units(half, [one.at[0, :, :, cols]], 4)
        up = remote(half, two.at[0, 0:4, :, cols], axis, nxt)
        hops[1].wait_recv()
        half = buf.at[prv * 2 + c, 4:8, :, cols]
        add_units(half, [one.at[1, :, :, cols]], 4)
        down = remote(half, two.at[1, 4:8, :, cols], axis, prv)
        return up, down, hops[2], hops[3]

    def own_block(buf, rc, core, cols, me):
        core[3].wait_recv()
        add_units(buf.at[me * 2 + c, :, :, cols], [rc.at[me, :, :, cols]], 8)

    def hop_last(buf, two, cols, hops, me):
        for copy in hops:
            copy.wait_recv()
        add_units(
            buf.at[me * 2 + c, :, :, cols],
            [two.at[0, :, :, cols], two.at[1, :, :, cols]], 8,
        )

    order_a, order_b = (zo, zp, zm, z), (xo, xp, xm, x)
    along_a, along_b = (Z, zo, zp, zm), (X, xo, xp, xm)
    core_b0 = core_part(gb, rcb, CUT_B[0], order_b)
    core_a0 = core_part(ga, rca, CUT_A[0], order_a)
    hops_b0 = hop_one(gb, rcb, core_b0, r1b, r2b, CUT_B[0], *along_b)
    core_b1 = core_part(gb, rcb, CUT_B[1], order_b)
    hops_a0 = hop_one(ga, rca, core_a0, r1a, r2a, CUT_A[0], *along_a)
    give_back(1)
    hops_b0 = hop_two(gb, r1b, r2b, CUT_B[0], hops_b0, X, xp, xm)
    hops_b1 = hop_one(gb, rcb, core_b1, r1b, r2b, CUT_B[1], *along_b)
    core_a1 = core_part(ga, rca, CUT_A[1], order_a)
    hops_a0 = hop_two(ga, r1a, r2a, CUT_A[0], hops_a0, Z, zp, zm)
    hops_a1 = hop_one(ga, rca, core_a1, r1a, r2a, CUT_A[1], *along_a)

    def pair_one(buf, block, q1, q2, cols, axis, opp, nxt, prv):
        def unit(k):
            return buf.at[block, k, :, cols]

        up = remote(unit(2 * opp), q1.at[0, :, cols], axis, nxt)
        down = remote(unit(2 * opp + 1), q1.at[1, :, cols], axis, prv)
        near_up = remote(unit(2 * nxt + 1), q2.at[0, 1, :, cols], axis, nxt)
        near_down = remote(unit(2 * prv), q2.at[1, 0, :, cols], axis, prv)
        return up, down, near_up, near_down

    def pair_two(buf, block, q1, q2, cols, hops, axis, nxt, prv):
        def add(k, src):
            total = buf[block, k, :, cols].astype(F32) + src[:, cols].astype(F32)
            buf[block, k, :, cols] = total.astype(BF16)
            return buf.at[block, k, :, cols]

        hops[0].wait_recv()
        up = remote(add(2 * nxt, q1.at[0]), q2.at[0, 0, :, cols], axis, nxt)
        hops[1].wait_recv()
        down = remote(add(2 * prv + 1, q1.at[1]), q2.at[1, 1, :, cols], axis, prv)
        return up, down, hops[2], hops[3]

    def pair_last(buf, block, q2, cols, hops, me):
        for copy in hops:
            copy.wait_recv()
        add_units(
            buf.at[block, pl.ds(2 * me, 2), :, cols],
            [q2.at[0, :, :, cols], q2.at[1, :, :, cols]], 2,
        )

    def returned(k):
        back[k].wait_recv()

        def step(r, carry):
            at = pl.ds(pl.multiple_of(k * IMG + r * 32, 32), 32)
            f[at, :] = (f[at, :].astype(F32) + frecv[at, :].astype(F32)).astype(BF16)
            return carry

        lax.fori_loop(0, 8, step, 0)
        outs.append(local(f.at[k * IMG:(k + 1) * IMG, 0:DINO], dino_grad.at[k, 0]))
        outs.append(local(f.at[k * IMG:(k + 1) * IMG, DINO:FEAT], siglip_grad.at[k, 0]))

    bias_c.wait_recv()
    bz[z] = bc[0] + bc[1]
    bias_z = [remote(bz.at[z], bz.at[z], Z, k) for k in (zp, zm, zo)]

    pair_a, pair_b = (za, q1a, q2a), (xb, q1b, q2b)
    own_block(gb, rcb, core_b0, CUT_B[0], x)
    own_block(ga, rca, core_a0, CUT_A[0], z)
    own_block(gb, rcb, core_b1, CUT_B[1], x)
    hops_b1 = hop_two(gb, r1b, r2b, CUT_B[1], hops_b1, X, xp, xm)
    hop_last(gb, r2b, CUT_B[0], hops_b0, x)
    hops_b0 = pair_one(gb, *pair_b, CUT_B[0], Z, zo, zp, zm)
    own_block(ga, rca, core_a1, CUT_A[1], z)
    hops_a1 = hop_two(ga, r1a, r2a, CUT_A[1], hops_a1, Z, zp, zm)
    hop_last(ga, r2a, CUT_A[0], hops_a0, z)
    hops_a0 = pair_one(ga, *pair_a, CUT_A[0], X, xo, xp, xm)

    feature_grad(0, 2 * IMG, f.at[0:2 * IMG])

    hop_last(gb, r2b, CUT_B[1], hops_b1, x)
    hops_b1 = pair_one(gb, *pair_b, CUT_B[1], Z, zo, zp, zm)
    hop_last(ga, r2a, CUT_A[1], hops_a1, z)
    hops_a1 = pair_one(ga, *pair_a, CUT_A[1], X, xo, xp, xm)
    hops_b0 = pair_two(gb, *pair_b, CUT_B[0], hops_b0, Z, zp, zm)
    hops_a0 = pair_two(ga, *pair_a, CUT_A[0], hops_a0, X, xp, xm)

    for copy in bias_z:
        copy.wait_recv()
    bx[x] = (bz[0] + bz[1]) + (bz[2] + bz[3])
    bias_x = [remote(bx.at[x], bx.at[x], X, k) for k in (xp, xm, xo)]

    hops_b1 = pair_two(gb, *pair_b, CUT_B[1], hops_b1, Z, zp, zm)
    hops_a1 = pair_two(ga, *pair_a, CUT_A[1], hops_a1, X, xp, xm)
    returned(0)
    for copy in bias_x:
        copy.wait_recv()
    by[y] = (bx[0] + bx[1]) + (bx[2] + bx[3])
    bias_y = remote(by.at[y], by.at[y], Y, yo)
    pair_last(gb, xb, q2b, CUT_B[0], hops_b0, z)
    pair_last(ga, za, q2a, CUT_A[0], hops_a0, x)
    pair_last(gb, xb, q2b, CUT_B[1], hops_b1, z)
    end_b = remote(gb.at[xb, 2 * z + yo], ryb, Y, yo)
    pair_last(ga, za, q2a, CUT_A[1], hops_a1, x)
    end_a = remote(ga.at[za, 2 * x + yo], rya, Y, yo)
    returned(1)

    end_a.wait_recv()
    wout[:, 0:WA] = ga[za, ua].astype(F32) + rya[...].astype(F32)
    end_b.wait_recv()
    wout[:, WA:FEAT] = gb[xb, ub].astype(F32) + ryb[...].astype(F32)
    outs.append(local(wout, wgrad))
    bias_y.wait_recv()
    flat_out[...] = (by[0] + by[1]).reshape(FEAT)
    outs.append(local(flat_out, bgrad))
    for copy in outs:
        copy.wait()
    wait_sends()


def handed_on(*refs):
    srcs, dsts, held, sem = refs[:5], refs[5:10], refs[10:15], refs[15]
    pieces = [(0, (b, slice(r * 128, (r + 1) * 128))) for b in range(2) for r in range(4)]
    pieces += [(k, b) for k in (3, 4) for b in range(2)] + [(1, ...), (2, ...)]

    def part(ref, at):
        return ref if at is ... else ref.at[at]

    ins, outs = [], []
    for n, (k, at) in enumerate(pieces):
        ins.append(pltpu.make_async_copy(part(srcs[k], at), part(held[k], at), sem.at[0, n]))
        outs.append(pltpu.make_async_copy(part(held[k], at), part(dsts[k], at), sem.at[1, n]))
    for copy in ins:
        copy.start()
    for fetched, copy in zip(ins, outs):
        fetched.wait()
        copy.start()
    for copy in outs:
        copy.wait()


def shards(dino_feats, siglip_feats, proj_weight, proj_bias, hidden_grad):
    vm = pltpu.VMEM
    unit_a, unit_b = (ROWS, WA), (ROWS, WB)
    scratch = [
        vm((8, 8, *unit_a), BF16), vm((8, 8, *unit_b), BF16),
        vm((FEAT, FEAT), BF16), vm((1024, FEAT), BF16), vm((FEAT, 1024), BF16),
        vm((1024, FEAT), BF16), vm((1024, FEAT), BF16), vm((512, FEAT), BF16),
        vm((512, FEAT), BF16),
        vm((4, 8, *unit_a), BF16), vm((4, 8, *unit_b), BF16),
        vm((2, 4, *unit_a), BF16), vm((2, 8, *unit_a), BF16),
        vm((2, 4, *unit_b), BF16), vm((2, 8, *unit_b), BF16),
        vm((2, *unit_a), BF16), vm((2, 2, *unit_a), BF16), vm(unit_a, BF16),
        vm((2, *unit_b), BF16), vm((2, 2, *unit_b), BF16), vm(unit_b, BF16),
        vm((GROUP, WB), F32), vm((512, 256), F32), vm((512, 256), F32), vm((ROWS, FEAT), F32),
        vm((1, FEAT), F32), vm((1, FEAT), F32),
        vm((2, 1, FEAT), F32), vm((4, 1, FEAT), F32), vm((4, 1, FEAT), F32),
        vm((2, 1, FEAT), F32), vm((FEAT,), F32), vm((FEAT,), F32),
        pltpu.SemaphoreType.DMA((COPIES,)), pltpu.SemaphoreType.DMA((COPIES,)),
        pltpu.SemaphoreType.DMA((LOCALS,)),
    ]
    anywhere = pl.BlockSpec(memory_space=pl.ANY)
    results = pl.pallas_call(
        kernel,
        out_shape=(
            jax.ShapeDtypeStruct(hidden_grad.shape, BF16),
            jax.ShapeDtypeStruct((ROWS, FEAT), F32),
            jax.ShapeDtypeStruct((FEAT,), F32),
            jax.ShapeDtypeStruct(dino_feats.shape, BF16),
            jax.ShapeDtypeStruct(siglip_feats.shape, BF16),
        ),
        in_specs=[anywhere] * 5,
        out_specs=[anywhere] * 5,
        scratch_shapes=scratch,
        compiler_params=pltpu.CompilerParams(
            collective_id=0, has_side_effects=True, vmem_limit_bytes=62 * 2**20
        ),
        cost_estimate=pl.CostEstimate(
            flops=6 * 1024 * FEAT * FEAT, bytes_accessed=20 * 2**20, transcendentals=4 * 2**20
        ),
    )(dino_feats, siglip_feats, proj_weight, proj_bias, hidden_grad)
    return pl.pallas_call(
        handed_on,
        out_shape=tuple(jax.ShapeDtypeStruct(r.shape, r.dtype) for r in results),
        in_specs=[anywhere] * 5,
        out_specs=[anywhere] * 5,
        scratch_shapes=[vm(r.shape, r.dtype) for r in results] + [pltpu.SemaphoreType.DMA((2, 14))],
        cost_estimate=pl.CostEstimate(flops=0, bytes_accessed=14 * 2**20, transcendentals=0),
    )(*results)


def solution(mesh):
    finer = Mesh(mesh.devices.reshape(mesh.shape["enc"], 4, 2, 4, 2), (E, *FSDP))
    in_specs = (
        P(FSDP, E, None, None), P(FSDP, E, None, None), P(FSDP, E), P(E), P(FSDP, None, E),
    )
    out_specs = (
        P(FSDP, None, E), P(FSDP, E), P(E), P(FSDP, E, None, None), P(FSDP, E, None, None),
    )
    return jax.shard_map(
        shards, mesh=finer, in_specs=in_specs, out_specs=out_specs, check_vma=False
    )
```

```python
import jax
import jax.numpy as jnp
from jax import lax
from jax.experimental import pallas as pl
from jax.experimental.pallas import tpu as pltpu
from jax.sharding import Mesh
from jax.sharding import PartitionSpec as P

E, X, Y, Z, C = "enc", "fsdp_0", "fsdp_1", "fsdp_2", "fsdp_3"
FSDP = (X, Y, Z, C)
DINO = 1024
SIG = 1152
FEAT = 2176
IMG = 256
ROWS = 34
WA = 1024
WB = 1152
GROUP = 8 * ROWS
F32 = jnp.float32
BF16 = jnp.bfloat16
CUT_A = (slice(0, 512), slice(512, WA))
CUT_B = (slice(0, 640), slice(640, WB))
COPIES = 136
LOCALS = 24


def kernel(
    dino, siglip, w, bias_in, hg,
    hidden, wgrad, bgrad, dino_grad, siglip_grad,
    ga, gb, wd, f, ft, lg, hid, fsend, frecv,
    rca, rcb, r1a, r2a, r1b, r2b, q1a, q2a, rya, q1b, q2b, ryb,
    scr, scr_next, pre, pre_next, wout, bias, bsum, bc, bz, bx, by, flat_in, flat_out,
    ssem, rsem, lsem,
):
    e, x, y, z, c = (lax.axis_index(n) for n in (E, X, Y, Z, C))
    xp, xm, xo = (lax.rem(x + k, 4) for k in (1, 3, 2))
    zp, zm, zo = (lax.rem(z + k, 4) for k in (1, 3, 2))
    yo, co, eo = 1 - y, 1 - c, 1 - e
    za, ua = z * 2 + c, x * 2 + y
    xb, ub = x * 2 + c, z * 2 + y

    counts = {"remote": 0, "local": 0}
    sends = []

    def remote(src, dst, axis, to):
        i = counts["remote"]
        counts["remote"] += 1
        copy = pltpu.make_async_remote_copy(
            src_ref=src, dst_ref=dst, send_sem=ssem.at[i], recv_sem=rsem.at[i],
            device_id={axis: to}, device_id_type=pl.DeviceIdType.MESH,
        )
        copy.start()
        sends.append(copy)
        return copy

    def local(src, dst):
        i = counts["local"]
        counts["local"] += 1
        copy = pltpu.make_async_copy(src, dst, lsem.at[i])
        copy.start()
        return copy

    def wait_sends():
        for copy in sends:
            copy.wait_send()
        sends.clear()

    own_w = [local(w.at[:, 0:WA], ga.at[za, ua]), local(w.at[:, WA:FEAT], gb.at[xb, ub])]
    own_f = []
    for b in range(2):
        own_f.append(local(dino.at[b, 0], f.at[b * IMG:(b + 1) * IMG, 0:DINO]))
        own_f.append(local(siglip.at[b, 0], f.at[b * IMG:(b + 1) * IMG, DINO:FEAT]))
    own_bias = local(bias_in, flat_in)

    barrier = pltpu.get_barrier_semaphore()
    peers = [(E, eo), (C, co), (Y, yo)]
    peers += [(X, k) for k in (xp, xm, xo)] + [(Z, k) for k in (zp, zm, zo)]
    for axis, to in peers:
        pl.semaphore_signal(
            barrier, inc=1, device_id={axis: to}, device_id_type=pl.DeviceIdType.MESH
        )
    pl.semaphore_wait(barrier, len(peers))

    for copy in own_w:
        copy.wait()
    def across(buf, block, unit):
        return remote(buf.at[block, unit], buf.at[block, unit], Y, yo)

    def near_pair(buf, block, me, axis, nxt, prv):
        pair = buf.at[block, pl.ds(2 * me, 2)]
        return remote(pair, pair, axis, nxt), remote(pair, pair, axis, prv)

    def far_pair(buf, block, hops, axis, nxt, prv):
        hops[0].wait_recv()
        unit = buf.at[block, 2 * prv]
        up = remote(unit, unit, axis, nxt)
        hops[1].wait_recv()
        unit = buf.at[block, 2 * nxt + 1]
        return up, remote(unit, unit, axis, prv)

    def near_block(buf, cols, me, axis, nxt, prv, shared):
        block = buf.at[me * 2 + c, :, :, cols]
        up, down = remote(block, block, axis, nxt), remote(block, block, axis, prv)
        shared.append(remote(block, block, C, co))
        return up, down

    def far_block(buf, cols, hops, axis, nxt, prv, shared):
        hops[0].wait_recv()
        block = buf.at[prv * 2 + c, :, :, cols]
        half = buf.at[prv * 2 + c, 0:4, :, cols]
        up = remote(half, half, axis, nxt)
        shared.append(remote(block, block, C, co))
        hops[1].wait_recv()
        block = buf.at[nxt * 2 + c, :, :, cols]
        half = buf.at[nxt * 2 + c, 4:8, :, cols]
        down = remote(half, half, axis, prv)
        shared.append(remote(block, block, C, co))
        return up, down

    def last_block(buf, cols, hops, opp, shared):
        for k, hop in enumerate(hops):
            hop.wait_recv()
            half = buf.at[opp * 2 + c, 4 * k:4 * k + 4, :, cols]
            shared.append(remote(half, half, C, co))

    def arrived(shared):
        for copy in shared:
            copy.wait_recv()

    shared = ([], [])
    across_a = across(ga, za, ua)
    across_b = across(gb, xb, ub)
    far_f = []
    for b in range(2):
        rows = slice(2 * IMG + b * IMG, 2 * IMG + (b + 1) * IMG)
        far_f.append(remote(dino.at[b, 0], f.at[rows, 0:DINO], E, eo))
        far_f.append(remote(siglip.at[b, 0], f.at[rows, DINO:FEAT], E, eo))
    del sends[-4:]
    own_hg = []
    for i, image in enumerate((e, eo)):
        for b in range(2):
            own_hg.append(
                local(
                    hg.at[b, pl.ds(pl.multiple_of(image * IMG, IMG), IMG)],
                    lg.at[(2 * i + b) * IMG:(2 * i + b + 1) * IMG],
                )
            )

    across_a.wait_recv()
    hops_a = near_pair(ga, za, x, X, xp, xm)
    across_b.wait_recv()
    hops_b = near_pair(gb, xb, z, Z, zp, zm)
    hops_a = far_pair(ga, za, hops_a, X, xp, xm)
    hops_b = far_pair(gb, xb, hops_b, Z, zp, zm)
    for hop in hops_a:
        hop.wait_recv()
    hops_a = near_block(ga, CUT_A[0], z, Z, zp, zm, shared[0])
    for hop in hops_b:
        hop.wait_recv()
    hops_b = near_block(gb, CUT_B[0], x, X, xp, xm, shared[0])

    def transposed(first, count):
        def step(t, carry):
            cols = pl.ds(pl.multiple_of(t * 128, 128), 128)
            ft[cols, first:first + count] = f[first:first + count, cols].T
            return carry
        lax.fori_loop(0, FEAT // 128, step, 0)

    for copy in own_f:
        copy.wait()
    transposed(0, 512)

    hops_a = far_block(ga, CUT_A[0], hops_a, Z, zp, zm, shared[0])
    then_a = near_block(ga, CUT_A[1], z, Z, zp, zm, shared[1])
    hops_b = far_block(gb, CUT_B[0], hops_b, X, xp, xm, shared[0])
    then_b = near_block(gb, CUT_B[1], x, X, xp, xm, shared[1])
    last_block(ga, CUT_A[0], hops_a, zo, shared[0])
    last_block(gb, CUT_B[0], hops_b, xo, shared[0])
    arrived(shared[0])

    def where_b(g, j):
        return (g // 2) * 2 + j % 2, (j // 2) * 2 + lax.rem(g, 2)

    def assembled(n):
        def step(g, carry):
            rows = pl.ds(pl.multiple_of(g * GROUP, 16), GROUP)
            cols = CUT_A[n]
            for j in range(8):
                scr[j * ROWS:(j + 1) * ROWS, 0:512] = ga[j, g, :, cols].astype(F32)
            wd[rows, cols] = scr[:, 0:512].astype(BF16)
            cols = CUT_B[n]
            width = cols.stop - cols.start
            for j in range(8):
                i, k = where_b(g, j)
                scr[j * ROWS:(j + 1) * ROWS, 0:width] = gb[i, k, :, cols].astype(F32)
            wd[rows, WA + cols.start:WA + cols.stop] = scr[:, 0:width].astype(BF16)
            return carry
        lax.fori_loop(0, 8, step, 0)

    assembled(0)

    bsum[...] = jnp.zeros_like(bsum)
    own_bias.wait()
    bias[...] = flat_in[...].reshape(1, FEAT)

    def forward(n, first, count):
        tiles = []
        for start, stop in (
            (CUT_A[n].start, CUT_A[n].stop), (WA + CUT_B[n].start, WA + CUT_B[n].stop)
        ):
            tiles += [slice(k, min(k + 256, stop)) for k in range(start, stop, 256)]
        slots = (pre, pre_next)

        def product(k):
            cols = tiles[k]
            slots[k % 2][0:count, 0:cols.stop - cols.start] = jnp.dot(
                f[first:first + count, :], wd[:, cols], preferred_element_type=F32
            )

        def activation(k):
            cols = tiles[k]
            width = cols.stop - cols.start
            slot = slots[k % 2]
            shift = bias[:, cols]
            acc = jnp.zeros((8, width), F32)
            for r in range(count // 16):
                at = slice(r * 16, (r + 1) * 16)
                lat = slice(first + r * 16, first + (r + 1) * 16)
                v = slot[at, 0:width] + shift
                cdf = 0.5 + 0.5 * lax.erf(v * 0.7071067811865476)
                pdf = jnp.exp(v * v * -0.5) * 0.3989422804014327
                hid[lat, cols] = (v * cdf).astype(BF16)
                grad = (lg[lat, cols].astype(F32) * (cdf + v * pdf)).astype(BF16)
                lg[lat, cols] = grad
                wide = grad.astype(F32)
                acc = acc + (wide[0:8] + wide[8:16])
            bsum[:, cols] += jnp.sum(acc, axis=0, keepdims=True)

        product(0)
        for k in range(len(tiles)):
            if k + 1 < len(tiles):
                product(k + 1)
            activation(k)

    def hidden_out(k):
        image = e if k < 2 else eo
        return local(
            hid.at[k * IMG:(k + 1) * IMG],
            hidden.at[k % 2, pl.ds(pl.multiple_of(image * IMG, IMG), IMG)],
        )

    def feature_part(first, count, dst, start, width):
        dst[:, pl.ds(start, width)] = lax.dot_general(
            lg[first:first + count, :], wd[pl.ds(start, width), :],
            (((1,), (1,)), ((), ())), preferred_element_type=F32,
        ).astype(BF16)

    def feature_grad(first, count, dst):
        def step(t, carry):
            feature_part(first, count, dst, pl.multiple_of(t * 512, 512), 512)
            return carry
        lax.fori_loop(0, 4, step, 0)
        feature_part(first, count, dst, 2048, 128)

    def give_back(k):
        rows = slice(k * IMG, (k + 1) * IMG)
        feature_grad((2 + k) * IMG, IMG, fsend.at[rows])
        back.append(remote(fsend.at[rows], frecv.at[rows], E, eo))

    outs, back = [], []
    own_hg[0].wait()
    own_hg[1].wait()
    forward(0, 0, 2 * IMG)
    hops_a = far_block(ga, CUT_A[1], then_a, Z, zp, zm, shared[1])
    hops_b = far_block(gb, CUT_B[1], then_b, X, xp, xm, shared[1])
    far_f[0].wait_recv()
    far_f[1].wait_recv()
    own_hg[2].wait()
    forward(0, 2 * IMG, IMG)
    last_block(ga, CUT_A[1], hops_a, zo, shared[1])
    last_block(gb, CUT_B[1], hops_b, xo, shared[1])
    transposed(2 * IMG, IMG)
    arrived(shared[1])
    gathered = list(sends)
    sends.clear()
    assembled(1)
    forward(1, 2 * IMG, IMG)
    outs.append(hidden_out(2))
    give_back(0)
    forward(1, 0, 2 * IMG)
    outs.append(hidden_out(0))
    outs.append(hidden_out(1))
    far_f[2].wait_recv()
    far_f[3].wait_recv()
    own_hg[3].wait()
    forward(0, 3 * IMG, IMG)
    forward(1, 3 * IMG, IMG)
    outs.append(hidden_out(3))
    transposed(3 * IMG, IMG)
    for copy in gathered:
        copy.wait_send()
    sends.extend(far_f)

    bc[c] = bsum[...]
    bias_c = remote(bc.at[c], bc.at[c], C, co)

    def weight_part(buf, cols):
        width = cols.stop - cols.start
        at = slice(cols.start + (WA if buf is gb else 0), cols.stop + (WA if buf is gb else 0))

        def product(g, slot):
            rows = pl.ds(pl.multiple_of(g * GROUP, 16), GROUP)
            slot[:, 0:width] = jnp.dot(ft[rows, :], lg[:, at], preferred_element_type=F32)

        def laid_out(g, slot):
            for j in range(8):
                i, k = where_b(g, j) if buf is gb else (j, g)
                buf[i, k, :, cols] = slot[j * ROWS:(j + 1) * ROWS, 0:width].astype(BF16)

        def step(p, carry):
            product(2 * p, scr)
            product(2 * p + 1, scr_next)
            laid_out(2 * p, scr)
            laid_out(2 * p + 1, scr_next)
            return carry

        lax.fori_loop(0, 4, step, 0)

    def core_part(buf, rc, cols, order):
        weight_part(buf, cols)
        return [
            remote(buf.at[k * 2 + co, :, :, cols], rc.at[k, :, :, cols], C, co) for k in order
        ]

    def add_units(dst, srcs, n):
        def step(k, carry):
            total = dst[k].astype(F32)
            for src in srcs:
                total = total + src[k].astype(F32)
            dst[k] = total.astype(BF16)
            return carry
        lax.fori_loop(0, n, step, 0)

    def hop_one(buf, rc, core, one, two, cols, axis, opp, nxt, prv):
        def block(k):
            return buf.at[k * 2 + c, :, :, cols]

        def part(ref, *at):
            return ref.at[(*at, slice(None), cols)]

        low, high = slice(0, 4), slice(4, 8)
        core[0].wait_recv()
        add_units(block(opp), [rc.at[opp, :, :, cols]], 8)
        up = remote(part(buf, opp * 2 + c, low), part(one, 0, slice(None)), axis, nxt)
        down = remote(part(buf, opp * 2 + c, high), part(one, 1, slice(None)), axis, prv)
        core[1].wait_recv()
        add_units(block(nxt), [rc.at[nxt, :, :, cols]], 8)
        near_up = remote(part(buf, nxt * 2 + c, high), part(two, 0, high), axis, nxt)
        core[2].wait_recv()
        add_units(block(prv), [rc.at[prv, :, :, cols]], 8)
        near_down = remote(part(buf, prv * 2 + c, low), part(two, 1, low), axis, prv)
        return up, down, near_up, near_down

    def hop_two(buf, one, two, cols, hops, axis, nxt, prv):
        hops[0].wait_recv()
        half = buf.at[nxt * 2 + c, 0:4, :, cols]
        add_units(half, [one.at[0, :, :, cols]], 4)
        up = remote(half, two.at[0, 0:4, :, cols], axis, nxt)
        hops[1].wait_recv()
        half = buf.at[prv * 2 + c, 4:8, :, cols]
        add_units(half, [one.at[1, :, :, cols]], 4)
        down = remote(half, two.at[1, 4:8, :, cols], axis, prv)
        return up, down, hops[2], hops[3]

    def own_block(buf, rc, core, cols, me):
        core[3].wait_recv()
        add_units(buf.at[me * 2 + c, :, :, cols], [rc.at[me, :, :, cols]], 8)

    def hop_last(buf, two, cols, hops, me):
        for copy in hops:
            copy.wait_recv()
        add_units(
            buf.at[me * 2 + c, :, :, cols],
            [two.at[0, :, :, cols], two.at[1, :, :, cols]], 8,
        )

    order_a, order_b = (zo, zp, zm, z), (xo, xp, xm, x)
    along_a, along_b = (Z, zo, zp, zm), (X, xo, xp, xm)
    core_b0 = core_part(gb, rcb, CUT_B[0], order_b)
    core_a0 = core_part(ga, rca, CUT_A[0], order_a)
    hops_b0 = hop_one(gb, rcb, core_b0, r1b, r2b, CUT_B[0], *along_b)
    core_b1 = core_part(gb, rcb, CUT_B[1], order_b)
    hops_a0 = hop_one(ga, rca, core_a0, r1a, r2a, CUT_A[0], *along_a)
    give_back(1)
    hops_b0 = hop_two(gb, r1b, r2b, CUT_B[0], hops_b0, X, xp, xm)
    hops_b1 = hop_one(gb, rcb, core_b1, r1b, r2b, CUT_B[1], *along_b)
    core_a1 = core_part(ga, rca, CUT_A[1], order_a)
    hops_a0 = hop_two(ga, r1a, r2a, CUT_A[0], hops_a0, Z, zp, zm)
    hops_a1 = hop_one(ga, rca, core_a1, r1a, r2a, CUT_A[1], *along_a)

    def pair_one(buf, block, q1, q2, cols, axis, opp, nxt, prv):
        def unit(k):
            return buf.at[block, k, :, cols]

        up = remote(unit(2 * opp), q1.at[0, :, cols], axis, nxt)
        down = remote(unit(2 * opp + 1), q1.at[1, :, cols], axis, prv)
        near_up = remote(unit(2 * nxt + 1), q2.at[0, 1, :, cols], axis, nxt)
        near_down = remote(unit(2 * prv), q2.at[1, 0, :, cols], axis, prv)
        return up, down, near_up, near_down

    def pair_two(buf, block, q1, q2, cols, hops, axis, nxt, prv):
        def add(k, src):
            total = buf[block, k, :, cols].astype(F32) + src[:, cols].astype(F32)
            buf[block, k, :, cols] = total.astype(BF16)
            return buf.at[block, k, :, cols]

        hops[0].wait_recv()
        up = remote(add(2 * nxt, q1.at[0]), q2.at[0, 0, :, cols], axis, nxt)
        hops[1].wait_recv()
        down = remote(add(2 * prv + 1, q1.at[1]), q2.at[1, 1, :, cols], axis, prv)
        return up, down, hops[2], hops[3]

    def pair_last(buf, block, q2, cols, hops, me):
        for copy in hops:
            copy.wait_recv()
        add_units(
            buf.at[block, pl.ds(2 * me, 2), :, cols],
            [q2.at[0, :, :, cols], q2.at[1, :, :, cols]], 2,
        )

    def returned(k):
        back[k].wait_recv()

        def step(r, carry):
            at = pl.ds(pl.multiple_of(k * IMG + r * 32, 32), 32)
            f[at, :] = (f[at, :].astype(F32) + frecv[at, :].astype(F32)).astype(BF16)
            return carry

        lax.fori_loop(0, 8, step, 0)
        outs.append(local(f.at[k * IMG:(k + 1) * IMG, 0:DINO], dino_grad.at[k, 0]))
        outs.append(local(f.at[k * IMG:(k + 1) * IMG, DINO:FEAT], siglip_grad.at[k, 0]))

    bias_c.wait_recv()
    bz[z] = bc[0] + bc[1]
    bias_z = [remote(bz.at[z], bz.at[z], Z, k) for k in (zp, zm, zo)]

    pair_a, pair_b = (za, q1a, q2a), (xb, q1b, q2b)
    own_block(gb, rcb, core_b0, CUT_B[0], x)
    own_block(ga, rca, core_a0, CUT_A[0], z)
    own_block(gb, rcb, core_b1, CUT_B[1], x)
    hops_b1 = hop_two(gb, r1b, r2b, CUT_B[1], hops_b1, X, xp, xm)
    hop_last(gb, r2b, CUT_B[0], hops_b0, x)
    hops_b0 = pair_one(gb, *pair_b, CUT_B[0], Z, zo, zp, zm)
    own_block(ga, rca, core_a1, CUT_A[1], z)
    hops_a1 = hop_two(ga, r1a, r2a, CUT_A[1], hops_a1, Z, zp, zm)
    hop_last(ga, r2a, CUT_A[0], hops_a0, z)
    hops_a0 = pair_one(ga, *pair_a, CUT_A[0], X, xo, xp, xm)

    feature_grad(0, 2 * IMG, f.at[0:2 * IMG])

    hop_last(gb, r2b, CUT_B[1], hops_b1, x)
    hops_b1 = pair_one(gb, *pair_b, CUT_B[1], Z, zo, zp, zm)
    hop_last(ga, r2a, CUT_A[1], hops_a1, z)
    hops_a1 = pair_one(ga, *pair_a, CUT_A[1], X, xo, xp, xm)
    hops_b0 = pair_two(gb, *pair_b, CUT_B[0], hops_b0, Z, zp, zm)
    hops_a0 = pair_two(ga, *pair_a, CUT_A[0], hops_a0, X, xp, xm)

    for copy in bias_z:
        copy.wait_recv()
    bx[x] = (bz[0] + bz[1]) + (bz[2] + bz[3])
    bias_x = [remote(bx.at[x], bx.at[x], X, k) for k in (xp, xm, xo)]

    hops_b1 = pair_two(gb, *pair_b, CUT_B[1], hops_b1, Z, zp, zm)
    hops_a1 = pair_two(ga, *pair_a, CUT_A[1], hops_a1, X, xp, xm)
    returned(0)
    for copy in bias_x:
        copy.wait_recv()
    by[y] = (bx[0] + bx[1]) + (bx[2] + bx[3])
    bias_y = remote(by.at[y], by.at[y], Y, yo)
    pair_last(gb, xb, q2b, CUT_B[0], hops_b0, z)
    pair_last(ga, za, q2a, CUT_A[0], hops_a0, x)
    pair_last(gb, xb, q2b, CUT_B[1], hops_b1, z)
    end_b = remote(gb.at[xb, 2 * z + yo], ryb, Y, yo)
    pair_last(ga, za, q2a, CUT_A[1], hops_a1, x)
    end_a = remote(ga.at[za, 2 * x + yo], rya, Y, yo)
    returned(1)

    end_a.wait_recv()
    wout[:, 0:WA] = ga[za, ua].astype(F32) + rya[...].astype(F32)
    end_b.wait_recv()
    wout[:, WA:FEAT] = gb[xb, ub].astype(F32) + ryb[...].astype(F32)
    outs.append(local(wout, wgrad))
    bias_y.wait_recv()
    flat_out[...] = (by[0] + by[1]).reshape(FEAT)
    outs.append(local(flat_out, bgrad))
    for copy in outs:
        copy.wait()
    wait_sends()


def handed_on(*refs):
    srcs, dsts, held, sem = refs[:5], refs[5:10], refs[10:15], refs[15]
    pieces = [(0, (b, slice(r * 128, (r + 1) * 128))) for b in range(2) for r in range(4)]
    pieces += [(k, b) for k in (3, 4) for b in range(2)] + [(1, ...), (2, ...)]

    def part(ref, at):
        return ref if at is ... else ref.at[at]

    ins, outs = [], []
    for n, (k, at) in enumerate(pieces):
        ins.append(pltpu.make_async_copy(part(srcs[k], at), part(held[k], at), sem.at[0, n]))
        outs.append(pltpu.make_async_copy(part(held[k], at), part(dsts[k], at), sem.at[1, n]))
    for copy in ins:
        copy.start()
    for fetched, copy in zip(ins, outs):
        fetched.wait()
        copy.start()
    for copy in outs:
        copy.wait()


def shards(dino_feats, siglip_feats, proj_weight, proj_bias, hidden_grad):
    vm = pltpu.VMEM
    unit_a, unit_b = (ROWS, WA), (ROWS, WB)
    scratch = [
        vm((8, 8, *unit_a), BF16), vm((8, 8, *unit_b), BF16),
        vm((FEAT, FEAT), BF16), vm((1024, FEAT), BF16), vm((FEAT, 1024), BF16),
        vm((1024, FEAT), BF16), vm((1024, FEAT), BF16), vm((512, FEAT), BF16),
        vm((512, FEAT), BF16),
        vm((4, 8, *unit_a), BF16), vm((4, 8, *unit_b), BF16),
        vm((2, 4, *unit_a), BF16), vm((2, 8, *unit_a), BF16),
        vm((2, 4, *unit_b), BF16), vm((2, 8, *unit_b), BF16),
        vm((2, *unit_a), BF16), vm((2, 2, *unit_a), BF16), vm(unit_a, BF16),
        vm((2, *unit_b), BF16), vm((2, 2, *unit_b), BF16), vm(unit_b, BF16),
        vm((GROUP, 640), F32), vm((GROUP, 640), F32), vm((512, 256), F32), vm((512, 256), F32), vm((ROWS, FEAT), F32),
        vm((1, FEAT), F32), vm((1, FEAT), F32),
        vm((2, 1, FEAT), F32), vm((4, 1, FEAT), F32), vm((4, 1, FEAT), F32),
        vm((2, 1, FEAT), F32), vm((FEAT,), F32), vm((FEAT,), F32),
        pltpu.SemaphoreType.DMA((COPIES,)), pltpu.SemaphoreType.DMA((COPIES,)),
        pltpu.SemaphoreType.DMA((LOCALS,)),
    ]
    anywhere = pl.BlockSpec(memory_space=pl.ANY)
    results = pl.pallas_call(
        kernel,
        out_shape=(
            jax.ShapeDtypeStruct(hidden_grad.shape, BF16),
            jax.ShapeDtypeStruct((ROWS, FEAT), F32),
            jax.ShapeDtypeStruct((FEAT,), F32),
            jax.ShapeDtypeStruct(dino_feats.shape, BF16),
            jax.ShapeDtypeStruct(siglip_feats.shape, BF16),
        ),
        in_specs=[anywhere] * 5,
        out_specs=[anywhere] * 5,
        scratch_shapes=scratch,
        compiler_params=pltpu.CompilerParams(
            collective_id=0, has_side_effects=True, vmem_limit_bytes=62 * 2**20
        ),
        cost_estimate=pl.CostEstimate(
            flops=6 * 1024 * FEAT * FEAT, bytes_accessed=20 * 2**20, transcendentals=4 * 2**20
        ),
    )(dino_feats, siglip_feats, proj_weight, proj_bias, hidden_grad)
    return pl.pallas_call(
        handed_on,
        out_shape=tuple(jax.ShapeDtypeStruct(r.shape, r.dtype) for r in results),
        in_specs=[anywhere] * 5,
        out_specs=[anywhere] * 5,
        scratch_shapes=[vm(r.shape, r.dtype) for r in results] + [pltpu.SemaphoreType.DMA((2, 14))],
        cost_estimate=pl.CostEstimate(flops=0, bytes_accessed=14 * 2**20, transcendentals=0),
    )(*results)


def solution(mesh):
    finer = Mesh(mesh.devices.reshape(mesh.shape["enc"], 4, 2, 4, 2), (E, *FSDP))
    in_specs = (
        P(FSDP, E, None, None), P(FSDP, E, None, None), P(FSDP, E), P(E), P(FSDP, None, E),
    )
    out_specs = (
        P(FSDP, None, E), P(FSDP, E), P(E), P(FSDP, E, None, None), P(FSDP, E, None, None),
    )
    return jax.shard_map(
        shards, mesh=finer, in_specs=in_specs, out_specs=out_specs, check_vma=False
    )
```
